128 devices in a mesh: band: 16 (over y, x), ga: 8 (over z, core).
Axes of the slice: x: 4, y: 4, z: 4, core: 2. Of those that a mesh axis runs over, the one named last changes fastest.
Arguments:
- waves: bfloat16 [2, 128, 4, 147456], P(None, 'band', None, 'ga'), as said below
- ionic_field: float32 [384, 1536], P('ga'), may hold values from -1 to 3
- point_charge: float32 [32768], P(('band', 'ga')), may hold values from -6 to 6
- charge_place: float32 [3, 32768], P(None, ('band', 'ga')), may hold values from 0 to 1
- charge_slab: int32 [32768, 1], P(('band', 'ga')), may hold values from 0 to 7; in each aligned block of 256 rows (0 to 255, 256 to 511, ...) at most 128 rows name the same one
Outputs:
- applied_waves: bfloat16 [2, 128, 4, 147456], P(None, 'band', None, 'ga')
- subspace: float32 [2, 128, 128], P(None, 'band', 'ga')
The draws below stay inside these ranges and needn't reach their ends.
Inputs may be any that keep to these rules, and one draw needn't show every extreme that they name: `waves`: entries are of order one. `charge_slab`: among the 256 rows of one device at most 128 name the same slab, and in every draw some device has exactly 128 rows naming one slab.
All inputs are finite; a program needn't handle non-finite values.
Results may differ from the reference program's by a relative error of at most 0.0073.
Values may be sent and summed in bfloat16 or wider, within the bound.
A program may use at most 128 MiB of HBM per device.

```python
import math
import jax
import jax.numpy as jnp
import numpy as np
from jax import lax

NX = 384
NY = 384
P_SIZE = 4
A_DEV = 256
NB = 128
SLAB = 48
NMM = 32768
N_GA = 8


def draw_waves(key, part):
    key = jax.random.fold_in(key, 7)
    key_base, key_first, key_second = jax.random.split(key, 3)
    shape_all = (2, NB, P_SIZE, NX * NY)
    base_draw = jnp.clip(jax.random.normal(key_base, shape_all, jnp.float32), -4.0, 4.0)
    first_order = jax.random.permutation(key_first, NB)
    second_order = jax.random.permutation(key_second, NB)
    mixed_one = base_draw[:, first_order]
    turned = base_draw[:, second_order]
    turned = jnp.stack([-turned[1], turned[0]])
    return (base_draw + 0.5 * mixed_one + 0.5 * turned).astype(jnp.bfloat16)


def level_of(own_key, extent, shards, least, high):
    factor_of, own = 1.0, jax.random.fold_in(own_key, 6)
    for axis_at, parts in shards:
        steps = jnp.exp(jax.random.uniform(jax.random.fold_in(own, axis_at), (parts,), jnp.float32, least / len(shards), high / len(shards)))
        factor_of = factor_of * jnp.repeat(steps, extent[axis_at] // parts).reshape([-1 if axis == axis_at else 1 for axis in range(len(extent))])
    return factor_of


def routed_block(own_key, own, number, rows, number_of, top, limit, slope):
    ranking = jax.random.permutation(own_key, number_of)
    heavy_load, usual = load_shares(number_of, rows * top, limit, slope, True), load_shares(number_of, rows * top, limit, slope, False)
    places = jnp.arange(number_of)

    def named(lengths, turn):
        used = int((lengths > 0).sum())
        fixed = max(1, used // 4)
        moved = fixed + (places - fixed + turn * (used - fixed)) % max(1, number_of - fixed)
        return jnp.zeros((number_of,), jnp.int32).at[ranking[jnp.where(places < fixed, places, moved)]].set(jnp.asarray(lengths, jnp.int32))

    lengths = jnp.where(number % 4 == 0, named(heavy_load, number // 4), named(usual, number - number // 4 - 1))
    mixed = jax.random.permutation(jax.random.fold_in(own, 3), number_of)
    donor, taker = mixed[0:number_of // 2 * 2:2], mixed[1:number_of // 2 * 2:2]
    slack = jnp.minimum(lengths[donor] - 1, limit - lengths[taker]) // 2
    slack = jnp.where((donor == ranking[0]) | (taker == ranking[0]) | (lengths[taker] == 0), 0, jnp.maximum(slack, 0))
    moved = jax.random.randint(jax.random.fold_in(own, 4), (number_of // 2,), 0, 1 << 20) % (slack + 1)
    lengths = lengths.at[donor].add(-moved).at[taker].add(moved)
    labels = jnp.searchsorted(jnp.cumsum(lengths), jnp.arange(rows * top), side="right").astype(jnp.int32)
    table = labels.reshape(top, rows).T
    table = table[jax.random.permutation(jax.random.fold_in(own, 1), rows)]
    turn = jax.random.randint(jax.random.fold_in(own, 2), (rows, 1), 0, top)
    return jnp.take_along_axis(table, (jnp.arange(top)[None, :] + turn) % top, axis=1)


def load_shares(count, total, reach, slope, full):
    weights = [(1 << 20) // math.isqrt(rank ** slope) + 1 for rank in range(1, count + 1)]
    largest = reach if full else min(reach, max(-(-total // count), total * weights[0] // sum(weights)))
    least = 1 if total - largest >= count - 1 else 0
    counts, spare = [largest] + [least] * (count - 1), total - largest - least * (count - 1)
    while spare > 0:
        movable = [i for i in range(1, count) if counts[i] < largest] or [i for i in range(1, count) if counts[i] < reach]
        pool, left = sum([weights[i] for i in movable]), spare
        for i in movable:
            extra = min(reach - counts[i], max(1, left * weights[i] // pool), spare)
            counts[i] = counts[i] + extra
            spare = spare - extra
    return np.array(counts)


def bell_draw(stream_key, dims, spread, limit, cuts=(), kind=jnp.bfloat16):
    values = jax.random.normal(stream_key, dims, jnp.float32) * spread
    if len(cuts) > 0:
        values = level_of(stream_key, dims, cuts, -0.22, 0.18) * values
    return jnp.clip(values, min=-limit, max=limit).astype(kind)


def setup_inputs(seed: int = 0) -> dict:
    keys = jax.random.split(jax.random.key(seed), 6)
    waves = draw_waves(jax.random.fold_in(keys[5], 71), 0)
    ionic_field = jnp.clip(-1.0 + 4.0 * jax.random.uniform(keys[1], (NY, P_SIZE * NX), jnp.float32) ** level_of(keys[1], (NY, P_SIZE * NX), ((0, 8),), -0.2, 0.2), -1.0, 3.0)
    point_charge = bell_draw(keys[2], (NMM,), 1.0, 6.0, ((0, 128),), jnp.float32)
    charge_place = jnp.clip(1.0 * jax.random.uniform(keys[3], (3, NMM), jnp.float32) ** level_of(keys[3], (3, NMM), ((1, 128),), -0.2, 0.2), 0.0, 1.0)
    charge_slab_keys = jax.random.split(jax.random.fold_in(keys[4], 1), NMM // A_DEV)
    charge_slab_turns = jax.random.permutation(jax.random.fold_in(keys[4], 3), NMM // A_DEV)
    charge_slab = jax.vmap(lambda own, number: routed_block(jax.random.fold_in(keys[4], 2), own, number, A_DEV, N_GA, 1, A_DEV // 2, 2))(charge_slab_keys, charge_slab_turns).reshape((NMM, 1))
    return {"waves": waves, "ionic_field": ionic_field, "point_charge": point_charge, "charge_place": charge_place, "charge_slab": charge_slab}


width_cells = 1.5

def tables(length):
    indices = jnp.arange(length, dtype=jnp.int32)
    phases = indices[:, None] * indices[None, :] % length
    angles = phases.astype(jnp.float32) * (2.0 * jnp.pi / length)
    factor = 1.0 / jnp.sqrt(jnp.float32(length))
    return jnp.stack([jnp.cos(angles) * factor, jnp.sin(angles) * factor]).astype(jnp.bfloat16)

def combine(products, sign_flip):
    return jnp.stack([products[0, 0] - sign_flip * products[1, 1], sign_flip * products[0, 1] + products[1, 0]])

def product_f32(form, left_side, right_side):
    return jnp.einsum(form, left_side.astype(jnp.float32), right_side.astype(jnp.float32), precision=lax.Precision.HIGHEST)

def gaussian(distance):
    return jnp.exp(-distance * distance / (2.0 * width_cells * width_cells))

def frequency(indices, length):
    return jnp.where(indices < length // 2, indices, indices - length).astype(jnp.float32)

def charge_field(point_charge, charge_place, charge_slab):
    target = charge_slab[:, 0]
    cells_x = jnp.arange(NX, dtype=jnp.float32)
    cells_y = jnp.arange(NY, dtype=jnp.float32)
    plane_cells = jnp.arange(P_SIZE, dtype=jnp.float32)
    along_y = target.astype(jnp.float32) * SLAB + SLAB * charge_place[1]
    kernel_x = gaussian(cells_x[None, :] - NX * charge_place[0][:, None])
    inside = jnp.arange(NY, dtype=jnp.int32)[None, :] // SLAB == target[:, None]
    kernel_y = gaussian(cells_y[None, :] - along_y[:, None]) * inside.astype(jnp.float32)
    kernel_z = gaussian(plane_cells[None, :] - P_SIZE * charge_place[2][:, None])
    right_side = ((point_charge[:, None] * kernel_z)[:, :, None] * kernel_x[:, None, :]).reshape(NMM, P_SIZE * NX)
    return jnp.dot(kernel_y.T, right_side, precision=lax.Precision.HIGHEST, preferred_element_type=jnp.float32)

def reference(waves, ionic_field, point_charge, charge_place, charge_slab):
    potential = (ionic_field + charge_field(point_charge, charge_place, charge_slab)).reshape(NY, P_SIZE, NX)
    table_rows = tables(NX)
    table_cols = tables(NY)
    freq_x = frequency(jnp.arange(NX, dtype=jnp.int32), NX)
    freq_y = frequency(jnp.arange(NY, dtype=jnp.int32), NY)
    kinetic = 2.0 * (freq_x[:, None] * freq_x[:, None] / (NX * NX) + freq_y[None, :] * freq_y[None, :] / (NY * NY))

    def apply_band(single_band):
        waves_grid = single_band.reshape(2, P_SIZE, NX, NY)
        half_done = combine(product_f32('cpxy,tyk->ctpxk', waves_grid, table_cols), 1.0).astype(jnp.bfloat16)
        in_space = combine(product_f32('cpxy,txk->ctypk', half_done, table_rows), 1.0)
        weighted = (potential * in_space).astype(jnp.bfloat16)
        return_half = combine(product_f32('cypx,txk->ctpyk', weighted, table_rows), -1.0).astype(jnp.bfloat16)
        recip_part = combine(product_f32('cpyx,tyk->ctpxk', return_half, table_cols), -1.0)
        applied = (kinetic * waves_grid.astype(jnp.float32) + recip_part).astype(jnp.bfloat16)
        return applied.reshape(2, P_SIZE, NX * NY)
    applied_waves = jnp.moveaxis(lax.map(apply_band, jnp.moveaxis(waves, 1, 0)), 0, 1)
    products = product_f32('cnpg,dmpg->cdnm', waves, applied_waves)
    inverse_cells = 1.0 / (P_SIZE * NX * NY)
    subspace = jnp.stack([products[0, 0] + products[1, 1], products[0, 1] - products[1, 0]]) * inverse_cells
    return (applied_waves, subspace)
```

```python
import functools

import jax
import jax.numpy as jnp
import ml_dtypes
import numpy as np
from jax import lax
from jax.experimental import pallas as pl
from jax.experimental.pallas import tpu as pltpu
from jax.sharding import PartitionSpec as P

N = 384
ROWS = 48
BF = jnp.bfloat16
F32 = jnp.float32
MESH = pl.DeviceIdType.MESH


def tables():
    indices = np.arange(N, dtype=np.int32)
    phases = indices[:, None] * indices[None, :] % N
    angles = phases.astype(np.float32) * np.float32(2.0 * np.pi / N)
    factor = np.float32(1.0) / np.sqrt(np.float32(N))
    return np.stack([np.cos(angles) * factor, np.sin(angles) * factor]).astype(ml_dtypes.bfloat16)


def dot(a, b):
    return jnp.dot(a, b, preferred_element_type=F32)


def dot_nt(a, b):
    return lax.dot_general(a, b, (((1,), (1,)), ((), ())), preferred_element_type=F32)


def split(value):
    high = value.astype(BF)
    return high, (value - high.astype(F32)).astype(BF)


def gaussian(distance):
    return jnp.exp(-distance * distance / 4.5)


def kernel(
    w1, charges, ionic, tab, out, sub,
    m1, m2, perm, kin, zb, w2, xw, phi, ph, p2, xp, ab, fs, ts, bs,
    ch, io, pot, rsb, pf, vyx, vxy, gt, sa, st, sb,
    zi_s, zi_r, zo_s, zo_r, ch_s, ch_r, io_s, io_r, rs_s, rs_r, ag_s, ag_r,
    sp_s, sp_r, sf_s, sf_r, xw_s, xw_r, xp_s, xp_r, sa_s, sa_r, sb_s, sb_r, loc,
):
    b = lax.axis_index("band")
    g = lax.axis_index("ga")
    z = g // 2
    h = lax.rem(g, 2)
    sibling = g + 1 - 2 * h

    def ga_peer(k):
        return lax.rem(g + k, 8)

    def band_peer(k):
        return lax.rem(b + k, 16)

    def remote(src, dst, send, recv, band, ga):
        return pltpu.make_async_remote_copy(
            src_ref=src, dst_ref=dst, send_sem=send, recv_sem=recv,
            device_id=(band, ga), device_id_type=MESH,
        )

    def at(start, size, step):
        return pl.ds(pl.multiple_of(start * size, step), size)

    barrier = pltpu.get_barrier_semaphore()

    def greet_ga(k, c):
        pl.semaphore_signal(barrier, inc=1, device_id=(b, ga_peer(k)), device_id_type=MESH)
        return c

    def greet_band(k, c):
        pl.semaphore_signal(barrier, inc=1, device_id=(band_peer(k), g), device_id_type=MESH)
        return c

    lax.fori_loop(1, 8, greet_ga, 0)
    lax.fori_loop(1, 16, greet_band, 0)
    pl.semaphore_wait(barrier, 22)

    def ch_copy(source, target):
        return remote(charges, ch.at[source], ch_s.at[target], ch_r.at[source], b, target)

    def io_copy(source, target):
        return remote(
            ionic.at[:, at(target // 2, N, 128)], io.at[at(source, ROWS, 8), :],
            io_s.at[target], io_r.at[source], b, target,
        )

    def zi_copy(n, source, target):
        return remote(
            w1.at[:, 4 * lax.rem(target, 2) + n, target // 2],
            zb.at[:, n, at(source, ROWS, 16), :],
            zi_s.at[n, target], zi_r.at[n, source], b, target,
        )

    def zo_copy(n, source, target):
        return remote(
            ab.at[:, n, at(target, ROWS, 16), :],
            out.at[:, 4 * lax.rem(source, 2) + n, source // 2],
            zo_s.at[n, target], zo_r.at[n, source], b, target,
        )

    def xw_copy(source, target):
        return remote(
            w2.at[at(target, 12, 1)], xw.at[:, at(source, 16, 16), :],
            xw_s.at[target], xw_r.at[source], target, g,
        )

    def xp_copy(source, target):
        return remote(
            p2.at[at(target, 12, 1)], xp.at[:, at(source, 16, 16), :],
            xp_s.at[target], xp_r.at[source], target, g,
        )

    def rs_copy(source, target):
        return remote(
            pot.at[at(target, 16, 8), :], rsb.at[source],
            rs_s.at[target], rs_r.at[source], target, g,
        )

    def ag_copy(source, target):
        piece = at(source, 16, 8)
        return remote(
            pf.at[h, piece, :], pf.at[h, piece, :],
            ag_s.at[target], ag_r.at[source], target, g,
        )

    def sp_copy(half):
        return remote(pf.at[half], pf.at[half], sp_s.at[0], sp_r.at[0], b, sibling)

    def sf_copy(n, core):
        return remote(
            phi.at[n, :, at(1 - core, 192, 16), :], ph.at[:, 4 * core + n],
            sf_s.at[n], sf_r.at[n], b, sibling,
        )

    def sa_copy(source, target):
        return remote(
            gt.at[at(target, 32, 8), :], sa.at[source],
            sa_s.at[target], sa_r.at[source], b, target,
        )

    def sb_copy(source, target):
        return remote(
            st.at[at(target, 16, 8), :], sb.at[source],
            sb_s.at[target], sb_r.at[source], target, g,
        )

    def each(low, high, body):
        def step(k, c):
            body(k)
            return c

        lax.fori_loop(low, high, step, 0)

    each(1, 8, lambda k: ch_copy(g, ga_peer(k)).start())
    each(1, 8, lambda k: zi_copy(0, g, ga_peer(k)).start())
    each(1, 8, lambda k: io_copy(g, ga_peer(k)).start())
    for n in range(1, 4):
        each(1, 8, lambda k, n=n: zi_copy(n, g, ga_peer(k)).start())

    def zi_own(n):
        return pltpu.make_async_copy(
            w1.at[:, 4 * h + n, z], zb.at[:, n, at(g, ROWS, 16), :], loc.at[n]
        )

    for n in range(4):
        zi_own(n).start()

    c = tab[0]
    s = tab[1]
    m1[0:N, 0:N] = c
    m1[0:N, N : 2 * N] = s
    m1[N : 2 * N, 0:N] = -s
    m1[N : 2 * N, N : 2 * N] = c
    m2[0:N, 0:N] = c
    m2[0:N, N : 2 * N] = -s
    m2[N : 2 * N, 0:N] = s
    m2[N : 2 * N, N : 2 * N] = c
    to = lax.broadcasted_iota(jnp.int32, (256, 256), 0)
    of = lax.broadcasted_iota(jnp.int32, (256, 256), 1)
    perm[...] = jnp.where(
        ((to >> 4) == (of & 15)) & ((to & 15) == (of >> 4)), 1.0, 0.0
    ).astype(BF)

    def frequency(indices):
        return jnp.where(indices < N // 2, indices, indices - N).astype(F32)

    fx = frequency(lax.broadcasted_iota(jnp.int32, (N, N), 0))
    fy = frequency(lax.broadcasted_iota(jnp.int32, (N, N), 1))
    kin[...] = 2.0 * (fx * fx / (N * N) + fy * fy / (N * N))

    for p in range(4):
        def turn(x, p=p):
            block = w1[:, :, p, at(x, 16, 16), :].reshape(256, N)
            turned = dot(perm[...], block).astype(BF).reshape(16, 16, N)
            w2[pl.ds(ROWS * p + 16 * x, 16)] = turned

        each(0, 3, turn)

    each(1, 8, lambda k: ch_copy(ga_peer(k), g).wait_recv())
    ch[g] = charges[...]
    pot[...] = jnp.zeros((256, N), F32)

    def add_charges(source):
        rows = ch[source]
        q, u, v, w, slab = (rows[i : i + 1] for i in range(5))
        r = lax.broadcasted_iota(jnp.int32, (256, 256), 0)
        y = 192 * h + 12 * (r >> 4) + (r & 15)
        weight = q * gaussian(z.astype(F32) - 4.0 * w)
        inside = ((y * 1366) >> 16).astype(F32) == slab
        gy = gaussian(y.astype(F32) - (slab * 48.0 + 48.0 * v)) * weight
        gy = jnp.where(inside, gy, 0.0)
        x = lax.broadcasted_iota(jnp.int32, (N, 256), 0).astype(F32)
        gx = gaussian(x - 384.0 * u)
        yh, yl = split(gy)
        xh, xl = split(gx)
        pot[...] += dot_nt(yh, xh) + (dot_nt(yh, xl) + dot_nt(yl, xh))

    each(0, 8, add_charges)
    each(1, 16, lambda k: rs_copy(b, band_peer(k)).start())

    def xw_own():
        return pltpu.make_async_copy(
            w2.at[at(b, 12, 1)], xw.at[:, at(b, 16, 16), :], loc.at[4]
        )

    xw_own().start()
    each(1, 4, lambda k: xw_copy(b, band_peer(k)).start())

    each(1, 16, lambda k: rs_copy(band_peer(k), b).wait_recv())
    piece = pot[at(b, 16, 8), :]
    for k in range(1, 16):
        piece = piece + rsb[band_peer(k)]
    pf[h, at(b, 16, 8), :] = piece
    each(1, 16, lambda k: ag_copy(b, band_peer(k)).start())
    each(4, 16, lambda k: xw_copy(b, band_peer(k)).start())
    each(1, 16, lambda k: ag_copy(band_peer(k), b).wait_recv())
    sp_copy(h).start()
    each(1, 8, lambda k: io_copy(ga_peer(k), g).wait_recv())
    io[at(g, ROWS, 8), :] = ionic[:, at(z, N, 128)]
    sp_copy(1 - h).wait_recv()
    for half in range(2):
        def place(q, half=half):
            two = pf[half, at(q, 32, 8), :]
            dst = pl.ds(pl.multiple_of(192 * half + 24 * q, 8), 24)
            vyx[dst, :] = io[dst, :] + jnp.concatenate([two[0:12], two[16:28]], axis=0)

        each(0, 8, place)
    vxy[...] = vyx[...].T

    def plane(n):
        each(1, 8, lambda k: zi_copy(n, ga_peer(k), g).wait_recv())
        zi_own(n).wait()
        both = jnp.concatenate([zb[0, n], zb[1, n]], axis=1)
        fs[0:N] = dot(both, m1[:, 0:N]).astype(BF)
        fs[N : 2 * N] = dot(both, m1[:, N : 2 * N]).astype(BF)
        for part in range(2):
            space = dot(m2[part * N : (part + 1) * N], fs[...])
            phi[n, part] = space.astype(BF)
            ts[part * N : (part + 1) * N] = (space * vxy[...]).astype(BF)
        sf_copy(n, h).start()
        for part in range(2):
            ph[part, 4 * h + n] = phi[n, part, at(h, 192, 16), :]
        for part in range(2):
            bs[:, part * N : (part + 1) * N] = dot(
                m1[part * N : (part + 1) * N], ts[...]
            ).astype(BF)
        for part in range(2):
            recip = dot(bs[...], m2[:, part * N : (part + 1) * N])
            ab[part, n] = (kin[...] * zb[part, n].astype(F32) + recip).astype(BF)
        each(1, 8, lambda k: zo_copy(n, g, ga_peer(k)).start())
        zo_own(n).start()

    def zo_own(n):
        return pltpu.make_async_copy(
            ab.at[:, n, at(g, ROWS, 16), :], out.at[:, 4 * h + n, z], loc.at[5 + n]
        )

    each(0, 4, plane)

    each(0, 4, lambda n: sf_copy(n, 1 - h).wait_recv())

    def turn_field(x):
        block = ph[:, :, at(x, 16, 16), :].reshape(256, N)
        p2[at(x, 16, 16)] = dot(perm[...], block).astype(BF).reshape(16, 16, N)

    each(0, 12, turn_field)

    def xp_own():
        return pltpu.make_async_copy(
            p2.at[at(b, 12, 1)], xp.at[:, at(b, 16, 16), :], loc.at[9]
        )

    each(1, 16, lambda k: xp_copy(b, band_peer(k)).start())
    xp_own().start()

    gt[...] = jnp.zeros((256, 256), F32)
    each(1, 16, lambda k: xw_copy(band_peer(k), b).wait_recv())
    xw_own().wait()

    def gram(rows, weight):
        gt[...] += dot_nt((rows.astype(F32) * weight).astype(BF), rows)

    def gram_waves(i):
        x = ROWS * g + lax.rem(12 * b + i, ROWS)
        gram(xw[i], kin[pl.ds(x, 1), :])

    each(0, 12, gram_waves)
    each(1, 16, lambda k: xp_copy(band_peer(k), b).wait_recv())
    xp_own().wait()
    each(0, 12, lambda i: gram(xp[i], vxy[pl.ds(192 * h + 12 * b + i, 1), :]))

    each(1, 8, lambda k: sa_copy(g, ga_peer(k)).start())
    total = gt[at(g, 32, 8), :]
    each(1, 8, lambda k: sa_copy(ga_peer(k), g).wait_recv())
    for k in range(1, 8):
        total = total + sa[ga_peer(k)]
    st[...] = jnp.concatenate([total, jnp.zeros((96, 256), F32)], axis=0).T
    each(1, 16, lambda k: sb_copy(b, band_peer(k)).start())
    block = st[at(b, 16, 8), :]
    each(1, 16, lambda k: sb_copy(band_peer(k), b).wait_recv())
    for k in range(1, 16):
        block = block + sb[band_peer(k)]
    row = lax.broadcasted_iota(jnp.int32, (128, 128), 0)
    col = lax.broadcasted_iota(jnp.int32, (128, 128), 1)
    lane = ((col >> 3) << 4) + (col & 7)
    valid = col < 16
    pick_re = jnp.where(valid & (row == lane), 1.0, 0.0)
    pick_im = jnp.where(valid & (row == lane + 8), 1.0, 0.0)

    def pick(rows, which):
        return jnp.dot(rows, which, precision=lax.Precision.HIGHEST, preferred_element_type=F32)

    inverse_cells = 1.0 / (4 * N * N)
    rr, ri = pick(block, pick_re), pick(block, pick_im)
    sub[0] = (rr[0:8] + ri[8:16]) * inverse_cells
    sub[1] = (ri[0:8] - rr[8:16]) * inverse_cells

    for n in range(4):
        each(1, 8, lambda k, n=n: zo_copy(n, ga_peer(k), g).wait_recv())
        each(1, 8, lambda k, n=n: zi_copy(n, g, ga_peer(k)).wait_send())
        each(1, 8, lambda k, n=n: zo_copy(n, g, ga_peer(k)).wait_send())
        zo_own(n).wait()
        sf_copy(n, h).wait_send()

    def ga_sent(k):
        ch_copy(g, ga_peer(k)).wait_send()
        io_copy(g, ga_peer(k)).wait_send()
        sa_copy(g, ga_peer(k)).wait_send()

    def band_sent(k):
        rs_copy(b, band_peer(k)).wait_send()
        ag_copy(b, band_peer(k)).wait_send()
        xw_copy(b, band_peer(k)).wait_send()
        xp_copy(b, band_peer(k)).wait_send()
        sb_copy(b, band_peer(k)).wait_send()

    each(1, 8, ga_sent)
    each(1, 16, band_sent)
    sp_copy(h).wait_send()


def shards(table, waves, ionic_field, point_charge, charge_place, charge_slab):
    w1 = waves.reshape(2, 8, 4, ROWS, N)
    charges = jnp.concatenate(
        [
            point_charge[None, :],
            charge_place,
            charge_slab.reshape(1, 256).astype(F32),
            jnp.zeros((3, 256), F32),
        ],
        axis=0,
    )
    dma = pltpu.SemaphoreType.DMA
    vmem = pltpu.VMEM
    out, sub = pl.pallas_call(
        kernel,
        out_shape=(
            jax.ShapeDtypeStruct((2, 8, 4, ROWS, N), BF),
            jax.ShapeDtypeStruct((2, 8, 128), F32),
        ),
        in_specs=[pl.BlockSpec(memory_space=pltpu.VMEM)] * 4,
        out_specs=(
            pl.BlockSpec(memory_space=pl.ANY),
            pl.BlockSpec(memory_space=pltpu.VMEM),
        ),
        scratch_shapes=[
            vmem((2 * N, 2 * N), BF),
            vmem((2 * N, 2 * N), BF),
            vmem((256, 256), BF),
            vmem((N, N), F32),
            vmem((2, 4, N, N), BF),
            vmem((192, 16, N), BF),
            vmem((12, 256, N), BF),
            vmem((4, 2, N, N), BF),
            vmem((2, 8, 192, N), BF),
            vmem((192, 16, N), BF),
            vmem((12, 256, N), BF),
            vmem((2, 4, N, N), BF),
            vmem((2 * N, N), BF),
            vmem((2 * N, N), BF),
            vmem((N, 2 * N), BF),
            vmem((8, 8, 256), F32),
            vmem((N, N), F32),
            vmem((256, N), F32),
            vmem((16, 16, N), F32),
            vmem((2, 256, N), F32),
            vmem((N, N), F32),
            vmem((N, N), F32),
            vmem((256, 256), F32),
            vmem((8, 32, 256), F32),
            vmem((256, 128), F32),
            vmem((16, 16, 128), F32),
            dma((4, 8)), dma((4, 8)),
            dma((4, 8)), dma((4, 8)),
            dma((8,)), dma((8,)),
            dma((8,)), dma((8,)),
            dma((16,)), dma((16,)),
            dma((16,)), dma((16,)),
            dma((1,)), dma((1,)),
            dma((4,)), dma((4,)),
            dma((16,)), dma((16,)),
            dma((16,)), dma((16,)),
            dma((8,)), dma((8,)),
            dma((16,)), dma((16,)),
            dma((10,)),
        ],
        compiler_params=pltpu.CompilerParams(
            collective_id=0, has_side_effects=True, vmem_limit_bytes=56 * 1024 * 1024
        ),
    )(w1, charges, ionic_field, table)
    return out.reshape(2, 8, 4, ROWS * N), sub[:, :, :16]


def solution(mesh):
    placed = (
        P(None, "band", None, "ga"),
        P("ga", None),
        P(("band", "ga")),
        P(None, ("band", "ga")),
        P(("band", "ga"), None),
    )
    mapped = jax.shard_map(
        shards,
        mesh=mesh,
        in_specs=(P(None, None, None),) + placed,
        out_specs=(P(None, "band", None, "ga"), P(None, "band", "ga")),
        check_vma=False,
    )
    return functools.partial(mapped, tables())
```

```python
import functools

import jax
import jax.numpy as jnp
import ml_dtypes
import numpy as np
from jax import lax
from jax.experimental import pallas as pl
from jax.experimental.pallas import tpu as pltpu
from jax.sharding import PartitionSpec as P

N = 384
ROWS = 48
BF = jnp.bfloat16
F32 = jnp.float32
MESH = pl.DeviceIdType.MESH


def tables():
    indices = np.arange(N, dtype=np.int32)
    phases = indices[:, None] * indices[None, :] % N
    angles = phases.astype(np.float32) * np.float32(2.0 * np.pi / N)
    factor = np.float32(1.0) / np.sqrt(np.float32(N))
    both = np.stack([np.cos(angles) * factor, np.sin(angles) * factor])
    return both.astype(ml_dtypes.bfloat16).astype(np.float32)


def dot(a, b):
    return jnp.dot(a, b, preferred_element_type=F32)


def dot_nt(a, b):
    return lax.dot_general(a, b, (((1,), (1,)), ((), ())), preferred_element_type=F32)


def split(value):
    high = value.astype(BF)
    return high, (value - high.astype(F32)).astype(BF)


def gaussian(distance):
    return jnp.exp(-distance * distance / 4.5)


SHIFTS = (
    (0, 1), (1, 0), (0, 3), (3, 0), (2, 2), (1, 1), (3, 3), (1, 3),
    (3, 1), (0, 2), (2, 0), (1, 2), (2, 1), (3, 2), (2, 3),
)
PARTS = 4
PART = 12 // PARTS


def each(low, high, body):
    def step(k, c):
        body(k)
        return c

    lax.fori_loop(low, high, step, 0)


def at(start, size, step):
    return pl.ds(pl.multiple_of(start * size, step), size)


def place_of(row):
    m = row >> 4
    plane = (m * 11) >> 5
    return ((row & 15) * 3 + m - 3 * plane) * 4 + plane


def kernel(
    waves, charge, place, slab_in, ionic, tab_in, out, sub,
    xin, w1, tab, spread, m1, m2, perm, kin, zb, w2, xw, phi, wide, ph, p2, xp, ab, fs, ts, bs,
    chs, ch, ios, iop, pot, rsb, own, pf, vyx, vxy, gt, sa, st, sb,
    zi_s, zi_r, zo_s, zo_r, ch_s, ch_r, io_s, io_r, rs_s, rs_r, ag_s, ag_r,
    sp_s, sp_r, sf_s, sf_r, xw_s, xw_r, xp_s, xp_r, sa_s, sa_r, sb_s, sb_r, loc,
):
    b = lax.axis_index("band")
    g = lax.axis_index("ga")
    z = g // 2
    h = lax.rem(g, 2)
    sibling = g + 1 - 2 * h
    b_y = b // 4
    b_x = lax.rem(b, 4)

    def ga_peer(k):
        return lax.rem(g + k, 8)

    def band_peer(k):
        return lax.rem(b + k, 16)

    def shifted(dy, dx):
        return lax.rem(b_y + dy, 4) * 4 + lax.rem(b_x + dx, 4)

    def remote(src, dst, send, recv, band, ga):
        return pltpu.make_async_remote_copy(
            src_ref=src, dst_ref=dst, send_sem=send, recv_sem=recv,
            device_id=(band, ga), device_id_type=MESH,
        )

    barrier = pltpu.get_barrier_semaphore()
    each(1, 8, lambda k: pl.semaphore_signal(
        barrier, inc=1, device_id=(b, ga_peer(k)), device_id_type=MESH))
    each(1, 16, lambda k: pl.semaphore_signal(
        barrier, inc=1, device_id=(band_peer(k), g), device_id_type=MESH))

    def load(n):
        return pltpu.make_async_copy(
            waves.at[:, pl.ds(2 * n, 2)], xin.at[:, pl.ds(2 * n, 2)], loc.at[n]
        )

    def load_tab():
        return pltpu.make_async_copy(tab_in, tab, loc.at[4])

    for n in range(4):
        load(n).start()
    load_tab().start()

    lead = lax.broadcasted_iota(jnp.int32, (192, 192), 0)
    last = lax.broadcasted_iota(jnp.int32, (192, 192), 1)
    spread[...] = jnp.where(last == place_of(lead), 1.0, 0.0).astype(BF)

    def to_planes(n):
        load(n).wait()
        for core in range(2):
            def block(x, core=core):
                both = jnp.concatenate(
                    [xin[c, 2 * n + core, at(x, 12, 12)].reshape(192, 128) for c in range(2)],
                    axis=1,
                )
                rows = dot(spread[...], both).astype(BF)
                for m in range(12):
                    for c in range(2):
                        w1[c, 2 * n + core, m // 3, at(x, 16, 16), m % 3 * 128 : m % 3 * 128 + 128] = (
                            rows[16 * m : 16 * m + 16, 128 * c : 128 * c + 128]
                        )

            each(0, 3, block)

    chs[0:1] = charge[...]
    chs[1:4] = place[...]
    chs[4:5] = slab_in[...].astype(F32)
    chs[5:8] = jnp.zeros((3, 256), F32)
    to_planes(0)
    pl.semaphore_wait(barrier, 22)

    def local(src, dst, sem):
        pltpu.make_async_copy(src, dst, sem).start()

    def await_bytes(like, sem):
        pltpu.make_async_copy(like, like, sem).wait()

    def ch_send(target):
        remote(chs, ch.at[g], ch_s.at[0], ch_r.at[0], b, target).start()

    io_sends = lax.rem(g, 4) == b_y
    io_half = g // 4
    io_source = 4 * h + b_y

    def io_copy(plane):
        return remote(
            ios.at[plane], iop, io_s.at[plane], io_r.at[0], b, 2 * plane + io_half
        )

    def zi_send(n, target):
        remote(
            w1.at[:, 2 * n + lax.rem(target, 2), target // 2],
            zb.at[:, n, at(g, ROWS, 16), :], zi_s.at[0], zi_r.at[n], b, target,
        ).start()

    def zo_send(n, target):
        remote(
            ab.at[:, n, at(target, ROWS, 16), :],
            out.at[:, 2 * n + h, z], zo_s.at[0], zo_r.at[n], b, target,
        ).start()

    def row_sends(q, src, dst, send, recv):
        def to(target):
            return src.at[pl.ds(12 * target + PART * q, PART)], dst.at[pl.ds(PART * q, PART), at(b, 16, 16), :]

        for dy, dx in SHIFTS:
            target = shifted(dy, dx)
            one, other = to(target)
            remote(one, other, send.at[0], recv.at[q], target, g).start()
        one, other = to(b)
        local(one, other, recv.at[q])

    def sp_copy(half):
        return remote(pf.at[half], pf.at[half], sp_s.at[0], sp_r.at[0], b, sibling)

    def sf_copy(n, core):
        return remote(
            phi.at[n, :, at(1 - core, 192, 16), :], ph.at[:, 2 * n + core],
            sf_s.at[0], sf_r.at[n], b, sibling,
        )

    each(1, 8, lambda k: ch_send(ga_peer(k)))
    local(chs, ch.at[g], ch_r.at[0])
    for n in range(4):
        if n:
            to_planes(n)
        each(1, 8, lambda k, n=n: zi_send(n, ga_peer(k)))
        local(w1.at[:, 2 * n + h, z], zb.at[:, n, at(g, ROWS, 16), :], zi_r.at[n])

    to = lax.broadcasted_iota(jnp.int32, (256, 256), 0)
    of = lax.broadcasted_iota(jnp.int32, (256, 256), 1)
    perm[...] = jnp.where(
        ((to >> 4) == (of & 15)) & ((to & 15) == (of >> 4)), 1.0, 0.0
    ).astype(BF)
    for p in range(4):
        def turn(x, p=p):
            block = w1[:, :, p, at(x, 16, 16), :].reshape(256, N)
            turned = dot(perm[...], block).astype(BF).reshape(16, 16, N)
            w2[pl.ds(ROWS * p + 16 * x, 16)] = turned

        each(0, 3, turn)

    def send_waves(q):
        row_sends(q, w2, xw, xw_s, xw_r)

    send_waves(0)

    @pl.when(io_sends)
    def _():
        for j in range(4):
            @pl.when(b_x == j)
            def _(j=j):
                for plane in range(4):
                    rows = ionic[12 * j : 12 * j + 12, plane * N : (plane + 1) * N]
                    ios[plane] = jnp.concatenate([rows, jnp.zeros((4, N), F32)], axis=0)
        for plane in range(4):
            @pl.when(2 * plane + io_half != g)
            def _(plane=plane):
                io_copy(plane).start()

    load_tab().wait()
    c = tab[0].astype(BF)
    s = tab[1].astype(BF)
    m1[0:N, 0:N] = c
    m1[0:N, N : 2 * N] = s
    m1[N : 2 * N, 0:N] = -s
    m1[N : 2 * N, N : 2 * N] = c
    m2[0:N, 0:N] = c
    m2[0:N, N : 2 * N] = -s
    m2[N : 2 * N, 0:N] = s
    m2[N : 2 * N, N : 2 * N] = c

    def frequency(indices):
        return jnp.where(indices < N // 2, indices, indices - N).astype(F32)

    fx = frequency(lax.broadcasted_iota(jnp.int32, (N, N), 0))
    fy = frequency(lax.broadcasted_iota(jnp.int32, (N, N), 1))
    kin[...] = 2.0 * (fx * fx / (N * N) + fy * fy / (N * N))

    await_bytes(ch, ch_r.at[0])
    pot[...] = jnp.zeros((256, N), F32)

    def add_charges(source):
        rows = ch[source]
        q, u, v, w, slab = (rows[i : i + 1] for i in range(5))
        r = lax.broadcasted_iota(jnp.int32, (256, 256), 0)
        y = 192 * h + 12 * (r >> 4) + (r & 15)
        weight = q * gaussian(z.astype(F32) - 4.0 * w)
        inside = ((y * 1366) >> 16).astype(F32) == slab
        gy = gaussian(y.astype(F32) - (slab * 48.0 + 48.0 * v)) * weight
        gy = jnp.where(inside, gy, 0.0)
        x = lax.broadcasted_iota(jnp.int32, (N, 256), 0).astype(F32)
        gx = gaussian(x - 384.0 * u)
        yh, yl = split(gy)
        xh, xl = split(gx)
        pot[...] += dot_nt(yh, xh) + (dot_nt(yh, xl) + dot_nt(yl, xh))

    each(0, 8, add_charges)

    def rs_send(target):
        remote(
            pot.at[at(target, 16, 8), :], rsb.at[b], rs_s.at[0], rs_r.at[0], target, g
        ).start()

    each(1, 16, lambda k: rs_send(band_peer(k)))
    local(pot.at[at(b, 16, 8), :], rsb.at[b], rs_r.at[0])
    for q in range(1, PARTS):
        send_waves(q)

    def forward(n):
        await_bytes(zb.at[:, n], zi_r.at[n])
        both = jnp.concatenate([zb[0, n], zb[1, n]], axis=1)
        fs[0:N] = dot(both, m1[:, 0:N]).astype(BF)
        fs[N : 2 * N] = dot(both, m1[:, N : 2 * N]).astype(BF)
        for part in range(2):
            space = dot(m2[part * N : (part + 1) * N], fs[...])
            wide[n, part] = space
            phi[n, part] = space.astype(BF)
        sf_copy(n, h).start()
        for part in range(2):
            ph[part, 2 * n + h] = phi[n, part, at(h, 192, 16), :]

    forward(0)

    await_bytes(rsb, rs_r.at[0])

    @pl.when(io_source == g)
    def _():
        iop[...] = ios[z]

    @pl.when(io_source != g)
    def _():
        io_copy(z).wait_recv()

    piece = iop[...]
    for k in range(16):
        piece = piece + rsb[k]
    own[...] = piece.astype(BF)

    def ag_send(target):
        remote(own, pf.at[h, at(b, 16, 16), :], ag_s.at[0], ag_r.at[0], target, g).start()

    each(1, 16, lambda k: ag_send(band_peer(k)))
    local(own, pf.at[h, at(b, 16, 16), :], ag_r.at[0])
    each(1, 4, forward)
    await_bytes(pf.at[h], ag_r.at[0])
    sp_copy(h).start()

    each(0, 4, lambda n: sf_copy(n, 1 - h).wait_recv())

    def turn_field(x):
        block = ph[:, :, at(x, 16, 16), :].reshape(256, N)
        p2[at(x, 16, 16)] = dot(perm[...], block).astype(BF).reshape(16, 16, N)

    each(0, 12, turn_field)
    for q in range(PARTS):
        row_sends(q, p2, xp, xp_s, xp_r)

    sp_copy(1 - h).wait_recv()
    for half in range(2):
        def join(q, half=half):
            two = pf[half, at(q, 32, 16), :].astype(F32)
            dst = pl.ds(pl.multiple_of(192 * half + 24 * q, 8), 24)
            vyx[dst, :] = jnp.concatenate([two[0:12], two[16:28]], axis=0)

        each(0, 8, join)
    vxy[...] = vyx[...].T

    def backward(n):
        for part in range(2):
            ts[part * N : (part + 1) * N] = (wide[n, part] * vxy[...]).astype(BF)
        for part in range(2):
            bs[:, part * N : (part + 1) * N] = dot(
                m1[part * N : (part + 1) * N], ts[...]
            ).astype(BF)
        for part in range(2):
            recip = dot(bs[...], m2[:, part * N : (part + 1) * N])
            ab[part, n] = (kin[...] * zb[part, n].astype(F32) + recip).astype(BF)
        each(1, 8, lambda k: zo_send(n, ga_peer(k)))
        local(ab.at[:, n, at(g, ROWS, 16), :], out.at[:, 2 * n + h, z], zo_r.at[n])

    each(0, 4, backward)

    def gram(data, q, weights):
        rows = [data[PART * q + i] for i in range(PART)]
        scaled = [(r.astype(F32) * w).astype(BF) for r, w in zip(rows, weights)]
        gt[...] += dot_nt(jnp.concatenate(scaled, axis=1), jnp.concatenate(rows, axis=1))

    gt[...] = jnp.zeros((256, 256), F32)

    def gram_waves(q):
        await_bytes(xw.at[pl.ds(PART * q, PART)], xw_r.at[q])
        x = [ROWS * g + lax.rem(12 * b + PART * q + i, ROWS) for i in range(PART)]
        gram(xw, q, [kin[pl.ds(i, 1), :] for i in x])

    each(0, PARTS, gram_waves)

    await_bytes(w1.at[:, pl.ds(0, 7)], zi_s.at[0])
    await_bytes(ph.at[:, pl.ds(0, 4)], sf_s.at[0])
    await_bytes(ch.at[pl.ds(0, 7)], ch_s.at[0])
    await_bytes(rsb.at[pl.ds(0, 15)], rs_s.at[0])
    await_bytes(pf.at[0, pl.ds(0, 240)], ag_s.at[0])
    await_bytes(w2.at[pl.ds(0, 180)], xw_s.at[0])
    sp_copy(h).wait_send()

    @pl.when(io_sends)
    def _():
        for plane in range(4):
            @pl.when(2 * plane + io_half != g)
            def _(plane=plane):
                io_copy(plane).wait_send()

    def finish(n):
        await_bytes(out.at[:, pl.ds(2 * n, 2)], zo_r.at[n])

    def gram_fields(q):
        await_bytes(xp.at[pl.ds(PART * q, PART)], xp_r.at[q])
        x = [192 * h + 12 * b + PART * q + i for i in range(PART)]
        gram(xp, q, [vxy[pl.ds(i, 1), :] for i in x])

    gram_fields(0)
    gram_fields(1)
    gram_fields(2)
    gram_fields(3)

    def sa_send(target):
        remote(
            gt.at[at(target, 32, 8), :], sa.at[g], sa_s.at[0], sa_r.at[0], b, target
        ).start()

    each(1, 8, lambda k: sa_send(ga_peer(k)))
    local(gt.at[at(g, 32, 8), :], sa.at[g], sa_r.at[0])
    await_bytes(p2.at[pl.ds(0, 180)], xp_s.at[0])
    finish(0)
    finish(1)
    await_bytes(sa, sa_r.at[0])
    total = sa[0]
    for k in range(1, 8):
        total = total + sa[k]
    st[...] = jnp.concatenate([total, jnp.zeros((96, 256), F32)], axis=0).T

    def sb_send(target):
        remote(
            st.at[at(target, 16, 8), :], sb.at[b], sb_s.at[0], sb_r.at[0], target, g
        ).start()

    each(1, 16, lambda k: sb_send(band_peer(k)))
    local(st.at[at(b, 16, 8), :], sb.at[b], sb_r.at[0])
    finish(2)
    finish(3)
    await_bytes(w1.at[:, pl.ds(0, 7)], zo_s.at[0])
    await_bytes(sa.at[pl.ds(0, 7)], sa_s.at[0])
    await_bytes(sb, sb_r.at[0])
    block = sb[0]
    for k in range(1, 16):
        block = block + sb[k]
    row = lax.broadcasted_iota(jnp.int32, (128, 128), 0)
    col = lax.broadcasted_iota(jnp.int32, (128, 128), 1)
    lane = ((col >> 3) << 4) + (col & 7)
    valid = col < 16
    pick_re = jnp.where(valid & (row == lane), 1.0, 0.0)
    pick_im = jnp.where(valid & (row == lane + 8), 1.0, 0.0)

    def pick(rows, which):
        return jnp.dot(rows, which, precision=lax.Precision.HIGHEST, preferred_element_type=F32)

    inverse_cells = 1.0 / (4 * N * N)
    rr, ri = pick(block, pick_re), pick(block, pick_im)
    sub[0] = ((rr[0:8] + ri[8:16]) * inverse_cells)[:, 0:16]
    sub[1] = ((ri[0:8] - rr[8:16]) * inverse_cells)[:, 0:16]

    await_bytes(sb.at[pl.ds(0, 15)], sb_s.at[0])


def shards(table, waves, ionic_field, point_charge, charge_place, charge_slab):
    tiled = waves.reshape(2, 8, 4, 144, 128).transpose(0, 1, 3, 2, 4).reshape(2, 8, 36, 16, 128)
    dma = pltpu.SemaphoreType.DMA
    vmem = pltpu.VMEM
    hbm = pl.BlockSpec(memory_space=pltpu.MemorySpace.HBM)
    out, sub = pl.pallas_call(
        kernel,
        out_shape=(
            jax.ShapeDtypeStruct((2, 8, 4, ROWS, N), BF),
            jax.ShapeDtypeStruct((2, 8, 16), F32),
        ),
        in_specs=[hbm] + [pl.BlockSpec(memory_space=pltpu.VMEM)] * 4 + [hbm],
        out_specs=(
            hbm,
            pl.BlockSpec(memory_space=pltpu.VMEM),
        ),
        scratch_shapes=[
            vmem((2, 8, 36, 16, 128), BF),
            vmem((2, 8, 4, ROWS, N), BF),
            vmem((2, N, N), F32),
            vmem((192, 192), BF),
            vmem((2 * N, 2 * N), BF),
            vmem((2 * N, 2 * N), BF),
            vmem((256, 256), BF),
            vmem((N, N), F32),
            vmem((2, 4, N, N), BF),
            vmem((192, 16, N), BF),
            vmem((12, 256, N), BF),
            vmem((4, 2, N, N), BF),
            vmem((4, 2, N, N), F32),
            vmem((2, 8, 192, N), BF),
            vmem((192, 16, N), BF),
            vmem((12, 256, N), BF),
            vmem((2, 4, N, N), BF),
            vmem((2 * N, N), BF),
            vmem((2 * N, N), BF),
            vmem((N, 2 * N), BF),
            vmem((8, 256), F32),
            vmem((8, 8, 256), F32),
            vmem((4, 16, N), F32),
            vmem((16, N), F32),
            vmem((256, N), F32),
            vmem((16, 16, N), F32),
            vmem((16, N), BF),
            vmem((2, 256, N), BF),
            vmem((N, N), F32),
            vmem((N, N), F32),
            vmem((256, 256), F32),
            vmem((8, 32, 256), F32),
            vmem((256, 128), F32),
            vmem((16, 16, 128), F32),
            dma((1,)), dma((4,)),
            dma((1,)), dma((4,)),
            dma((1,)), dma((1,)),
            dma((4,)), dma((1,)),
            dma((1,)), dma((1,)),
            dma((1,)), dma((1,)),
            dma((1,)), dma((1,)),
            dma((1,)), dma((4,)),
            dma((1,)), dma((PARTS,)),
            dma((1,)), dma((PARTS,)),
            dma((1,)), dma((1,)),
            dma((1,)), dma((1,)),
            dma((5,)),
        ],
        compiler_params=pltpu.CompilerParams(
            collective_id=0, has_side_effects=True, vmem_limit_bytes=56 * 1024 * 1024
        ),
    )(
        tiled, point_charge.reshape(1, 256), charge_place, charge_slab.reshape(1, 256),
        ionic_field, table,
    )
    return out.reshape(2, 8, 4, ROWS * N), sub


def solution(mesh):
    placed = (
        P(None, "band", None, "ga"),
        P("ga", None),
        P(("band", "ga")),
        P(None, ("band", "ga")),
        P(("band", "ga"), None),
    )
    mapped = jax.shard_map(
        shards,
        mesh=mesh,
        in_specs=(P(None, None, None),) + placed,
        out_specs=(P(None, "band", None, "ga"), P(None, "band", "ga")),
        check_vma=False,
    )
    return functools.partial(mapped, tables())
```

```python
import functools

import jax
import jax.numpy as jnp
import ml_dtypes
import numpy as np
from jax import lax
from jax.experimental import pallas as pl
from jax.experimental.pallas import tpu as pltpu
from jax.sharding import PartitionSpec as P

N = 384
ROWS = 48
BF = jnp.bfloat16
F32 = jnp.float32
MESH = pl.DeviceIdType.MESH


def tables():
    indices = np.arange(N, dtype=np.int32)
    phases = indices[:, None] * indices[None, :] % N
    angles = phases.astype(np.float32) * np.float32(2.0 * np.pi / N)
    factor = np.float32(1.0) / np.sqrt(np.float32(N))
    both = np.stack([np.cos(angles) * factor, np.sin(angles) * factor])
    return both.astype(ml_dtypes.bfloat16).astype(np.float32)


def dot(a, b):
    return jnp.dot(a, b, preferred_element_type=F32)


def dot_nt(a, b):
    return lax.dot_general(a, b, (((1,), (1,)), ((), ())), preferred_element_type=F32)


def split(value):
    high = value.astype(BF)
    return high, (value - high.astype(F32)).astype(BF)


def gaussian(distance):
    return jnp.exp(-distance * distance / 4.5)


SHIFTS = (
    (0, 1), (1, 0), (0, 3), (3, 0), (2, 2), (1, 1), (3, 3), (1, 3),
    (3, 1), (0, 2), (2, 0), (1, 2), (2, 1), (3, 2), (2, 3),
)
PARTS = 4
PART = 12 // PARTS


def each(low, high, body):
    def step(k, c):
        body(k)
        return c

    lax.fori_loop(low, high, step, 0)


def at(start, size, step):
    return pl.ds(pl.multiple_of(start * size, step), size)


def place_of(row):
    m = row >> 4
    plane = (m * 11) >> 5
    return ((row & 15) * 3 + m - 3 * plane) * 4 + plane


def kernel(
    waves, charge, place, slab_in, ionic, tab_in, out, sub,
    xin, w1, tab, rows_in, xout, spread, gather, m1, m2, perm, kin, zb, w2, xw, phi, wide, ph, p2, xp, ab, fs, ts, bs,
    chs, ch, ios, iop, pot, rsb, own, pf, vyx, vxy, gt, gb, sa, st, sb,
    zi_s, zi_r, zo_s, zo_r, ch_s, ch_r, io_s, io_r, rs_s, rs_r, ag_s, ag_r,
    sp_s, sp_r, sf_s, sf_r, xw_s, xw_r, xp_s, xp_r, sa_s, sa_r, sb_s, sb_r, loc, st_s,
):
    b = lax.axis_index("band")
    g = lax.axis_index("ga")
    z = g // 2
    h = lax.rem(g, 2)
    sibling = g + 1 - 2 * h
    b_y = b // 4
    b_x = lax.rem(b, 4)

    def ga_peer(k):
        return lax.rem(g + k, 8)

    def band_peer(k):
        return lax.rem(b + k, 16)

    def shifted(dy, dx):
        return lax.rem(b_y + dy, 4) * 4 + lax.rem(b_x + dx, 4)

    def remote(src, dst, send, recv, band, ga):
        return pltpu.make_async_remote_copy(
            src_ref=src, dst_ref=dst, send_sem=send, recv_sem=recv,
            device_id=(band, ga), device_id_type=MESH,
        )

    barrier = pltpu.get_barrier_semaphore()
    each(1, 8, lambda k: pl.semaphore_signal(
        barrier, inc=1, device_id=(b, ga_peer(k)), device_id_type=MESH))
    each(1, 16, lambda k: pl.semaphore_signal(
        barrier, inc=1, device_id=(band_peer(k), g), device_id_type=MESH))

    def load(n):
        return pltpu.make_async_copy(
            waves.at[:, pl.ds(2 * n, 2)], xin.at[:, pl.ds(2 * n, 2)], loc.at[n]
        )

    def load_tab():
        return pltpu.make_async_copy(tab_in, tab, loc.at[4])

    for n in range(4):
        load(n).start()
    load_tab().start()

    lead = lax.broadcasted_iota(jnp.int32, (192, 192), 0)
    last = lax.broadcasted_iota(jnp.int32, (192, 192), 1)
    spread[...] = jnp.where(last == place_of(lead), 1.0, 0.0).astype(BF)
    gather[...] = jnp.where(lead == place_of(last), 1.0, 0.0).astype(BF)

    def to_planes(n):
        load(n).wait()
        for core in range(2):
            for x in range(3):
                both = jnp.concatenate(
                    [xin[c, 2 * n + core, 12 * x : 12 * x + 12].reshape(192, 128) for c in range(2)],
                    axis=1,
                )
                rows = dot(spread[...], both).astype(BF)
                for m in range(12):
                    part = m % 3 * 128
                    for c in range(2):
                        w1[c, 2 * n + core, m // 3, 16 * x : 16 * x + 16, part : part + 128] = (
                            rows[16 * m : 16 * m + 16, 128 * c : 128 * c + 128]
                        )

    def from_planes(n):
        for core in range(2):
            for x in range(3):
                both = jnp.concatenate(
                    [
                        jnp.concatenate(
                            [
                                rows_in[
                                    c, 2 * n + core, m // 3, 16 * x : 16 * x + 16,
                                    m % 3 * 128 : m % 3 * 128 + 128,
                                ]
                                for m in range(12)
                            ],
                            axis=0,
                        )
                        for c in range(2)
                    ],
                    axis=1,
                )
                rows = dot(gather[...], both).astype(BF)
                for c in range(2):
                    xout[c, 2 * n + core, 12 * x : 12 * x + 12] = rows[
                        :, 128 * c : 128 * c + 128
                    ].reshape(12, 16, 128)

    chs[0:1] = charge[...]
    chs[1:4] = place[...]
    chs[4:5] = slab_in[...].astype(F32)
    chs[5:8] = jnp.zeros((3, 256), F32)
    each(0, 4, to_planes)

    to = lax.broadcasted_iota(jnp.int32, (256, 256), 0)
    of = lax.broadcasted_iota(jnp.int32, (256, 256), 1)
    perm[...] = jnp.where(
        ((to >> 4) == (of & 15)) & ((to & 15) == (of >> 4)), 1.0, 0.0
    ).astype(BF)
    def turn(p):
        for x in range(3):
            block = w1[:, :, p, 16 * x : 16 * x + 16, :].reshape(256, N)
            turned = dot(perm[...], block).astype(BF).reshape(16, 16, N)
            w2[pl.ds(ROWS * p + 16 * x, 16)] = turned

    each(0, 4, turn)
    pl.semaphore_wait(barrier, 22)

    def local(src, dst, sem):
        pltpu.make_async_copy(src, dst, sem).start()

    def await_bytes(like, sem):
        pltpu.make_async_copy(like, like, sem).wait()

    def ch_send(target):
        remote(chs, ch.at[g], ch_s.at[0], ch_r.at[0], b, target).start()

    io_sends = lax.rem(g, 4) == b_y
    io_half = g // 4
    io_source = 4 * h + b_y

    def io_copy(plane):
        return remote(
            ios.at[plane], iop, io_s.at[plane], io_r.at[0], b, 2 * plane + io_half
        )

    def zi_send(n, target):
        remote(
            w1.at[:, 2 * n + lax.rem(target, 2), target // 2],
            zb.at[:, n, at(g, ROWS, 16), :], zi_s.at[0], zi_r.at[n], b, target,
        ).start()

    def zo_send(n, target):
        remote(
            ab.at[:, n, at(target, ROWS, 16), :],
            rows_in.at[:, 2 * n + h, z], zo_s.at[0], zo_r.at[n], b, target,
        ).start()

    def row_sends(q, src, dst, send, recv):
        def to(target):
            return src.at[pl.ds(12 * target + PART * q, PART)], dst.at[pl.ds(PART * q, PART), at(b, 16, 16), :]

        for dy, dx in SHIFTS:
            target = shifted(dy, dx)
            one, other = to(target)
            remote(one, other, send.at[0], recv.at[q], target, g).start()
        one, other = to(b)
        local(one, other, recv.at[q])

    def sp_copy(half):
        return remote(pf.at[half], pf.at[half], sp_s.at[0], sp_r.at[0], b, sibling)

    def sf_copy(n, core):
        return remote(
            phi.at[n, :, at(1 - core, 192, 16), :], ph.at[:, 2 * n + core],
            sf_s.at[0], sf_r.at[n], b, sibling,
        )

    each(1, 8, lambda k: ch_send(ga_peer(k)))
    local(chs, ch.at[g], ch_r.at[0])
    def zi_all(n):
        each(1, 8, lambda k: zi_send(n, ga_peer(k)))
        local(w1.at[:, 2 * n + h, z], zb.at[:, n, at(g, ROWS, 16), :], zi_r.at[n])

    zi_all(0)

    def send_waves(q):
        row_sends(q, w2, xw, xw_s, xw_r)

    send_waves(0)
    send_waves(1)
    each(1, 4, zi_all)

    @pl.when(io_sends)
    def _():
        for j in range(4):
            @pl.when(b_x == j)
            def _(j=j):
                for plane in range(4):
                    rows = ionic[12 * j : 12 * j + 12, plane * N : (plane + 1) * N]
                    ios[plane] = jnp.concatenate([rows, jnp.zeros((4, N), F32)], axis=0)
        for plane in range(4):
            @pl.when(2 * plane + io_half != g)
            def _(plane=plane):
                io_copy(plane).start()

    load_tab().wait()
    c = tab[0].astype(BF)
    s = tab[1].astype(BF)
    m1[0:N, 0:N] = c
    m1[0:N, N : 2 * N] = s
    m1[N : 2 * N, 0:N] = -s
    m1[N : 2 * N, N : 2 * N] = c
    m2[0:N, 0:N] = c
    m2[0:N, N : 2 * N] = -s
    m2[N : 2 * N, 0:N] = s
    m2[N : 2 * N, N : 2 * N] = c

    def frequency(indices):
        return jnp.where(indices < N // 2, indices, indices - N).astype(F32)

    fx = frequency(lax.broadcasted_iota(jnp.int32, (N, N), 0))
    fy = frequency(lax.broadcasted_iota(jnp.int32, (N, N), 1))
    kin[...] = 2.0 * (fx * fx / (N * N) + fy * fy / (N * N))

    await_bytes(ch, ch_r.at[0])
    pot[...] = jnp.zeros((256, N), F32)

    def add_charges(source):
        rows = ch[source]
        q, u, v, w, slab = (rows[i : i + 1] for i in range(5))
        r = lax.broadcasted_iota(jnp.int32, (256, 256), 0)
        y = 192 * h + 12 * (r >> 4) + (r & 15)
        weight = q * gaussian(z.astype(F32) - 4.0 * w)
        inside = ((y * 1366) >> 16).astype(F32) == slab
        gy = gaussian(y.astype(F32) - (slab * 48.0 + 48.0 * v)) * weight
        gy = jnp.where(inside, gy, 0.0)
        x = lax.broadcasted_iota(jnp.int32, (N, 256), 0).astype(F32)
        gx = gaussian(x - 384.0 * u)
        yh, yl = split(gy)
        xh, xl = split(gx)
        pot[...] += dot_nt(yh, xh) + (dot_nt(yh, xl) + dot_nt(yl, xh))

    def add_two(i):
        add_charges(2 * i)
        add_charges(2 * i + 1)

    each(0, 4, add_two)

    def rs_send(target):
        remote(
            pot.at[at(target, 16, 8), :], rsb.at[b], rs_s.at[0], rs_r.at[0], target, g
        ).start()

    each(1, 16, lambda k: rs_send(band_peer(k)))
    local(pot.at[at(b, 16, 8), :], rsb.at[b], rs_r.at[0])
    send_waves(2)

    def forward(n):
        await_bytes(zb.at[:, n], zi_r.at[n])
        both = jnp.concatenate([zb[0, n], zb[1, n]], axis=1)
        fs[0:N] = dot(both, m1[:, 0:N]).astype(BF)
        fs[N : 2 * N] = dot(both, m1[:, N : 2 * N]).astype(BF)
        for part in range(2):
            space = dot(m2[part * N : (part + 1) * N], fs[...])
            wide[n, part] = space
            phi[n, part] = space.astype(BF)
        sf_copy(n, h).start()
        for part in range(2):
            ph[part, 2 * n + h] = phi[n, part, at(h, 192, 16), :]

    each(0, 2, forward)

    await_bytes(rsb, rs_r.at[0])

    @pl.when(io_source == g)
    def _():
        iop[...] = ios[z]

    @pl.when(io_source != g)
    def _():
        io_copy(z).wait_recv()

    piece = iop[...]
    for k in range(16):
        piece = piece + rsb[k]
    own[...] = piece.astype(BF)

    def ag_send(target):
        remote(own, pf.at[h, at(b, 16, 16), :], ag_s.at[0], ag_r.at[0], target, g).start()

    each(1, 16, lambda k: ag_send(band_peer(k)))
    local(own, pf.at[h, at(b, 16, 16), :], ag_r.at[0])
    send_waves(3)
    each(2, 4, forward)
    await_bytes(pf.at[h], ag_r.at[0])
    sp_copy(h).start()

    each(0, 4, lambda n: sf_copy(n, 1 - h).wait_recv())

    def turn_field(p):
        for x in range(3):
            block = ph[:, :, at(3 * p + x, 16, 16), :].reshape(256, N)
            p2[at(3 * p + x, 16, 16)] = dot(perm[...], block).astype(BF).reshape(16, 16, N)

    each(0, 4, turn_field)
    for q in range(PARTS):
        row_sends(q, p2, xp, xp_s, xp_r)

    sp_copy(1 - h).wait_recv()
    for half in range(2):
        def join(q, half=half):
            two = pf[half, at(q, 32, 16), :].astype(F32)
            dst = pl.ds(pl.multiple_of(192 * half + 24 * q, 8), 24)
            vyx[dst, :] = jnp.concatenate([two[0:12], two[16:28]], axis=0)

        each(0, 8, join)
    vxy[...] = vyx[...].T

    def backward(n):
        for part in range(2):
            ts[part * N : (part + 1) * N] = (wide[n, part] * vxy[...]).astype(BF)
        for part in range(2):
            bs[:, part * N : (part + 1) * N] = dot(
                m1[part * N : (part + 1) * N], ts[...]
            ).astype(BF)
        for part in range(2):
            recip = dot(bs[...], m2[:, part * N : (part + 1) * N])
            ab[part, n] = (kin[...] * zb[part, n].astype(F32) + recip).astype(BF)
        each(1, 8, lambda k: zo_send(n, ga_peer(k)))
        local(ab.at[:, n, at(g, ROWS, 16), :], rows_in.at[:, 2 * n + h, z], zo_r.at[n])

    each(0, 4, backward)

    def gram(data, q, weights):
        rows = [data[PART * q + i] for i in range(PART)]
        scaled = [(r.astype(F32) * w).astype(BF) for r, w in zip(rows, weights)]
        gt[...] += dot_nt(jnp.concatenate(rows, axis=1), jnp.concatenate(scaled, axis=1))

    gt[...] = jnp.zeros((256, 256), F32)

    def gram_waves(q):
        await_bytes(xw.at[pl.ds(PART * q, PART)], xw_r.at[q])
        x = [ROWS * g + lax.rem(12 * b + PART * q + i, ROWS) for i in range(PART)]
        gram(xw, q, [kin[pl.ds(i, 1), :] for i in x])

    each(0, PARTS, gram_waves)

    await_bytes(w1.at[:, pl.ds(0, 7)], zi_s.at[0])
    await_bytes(ph.at[:, pl.ds(0, 4)], sf_s.at[0])
    await_bytes(ch.at[pl.ds(0, 7)], ch_s.at[0])
    await_bytes(rsb.at[pl.ds(0, 15)], rs_s.at[0])
    await_bytes(pf.at[0, pl.ds(0, 240)], ag_s.at[0])
    await_bytes(w2.at[pl.ds(0, 180)], xw_s.at[0])
    sp_copy(h).wait_send()

    @pl.when(io_sends)
    def _():
        for plane in range(4):
            @pl.when(2 * plane + io_half != g)
            def _(plane=plane):
                io_copy(plane).wait_send()

    def finish(n):
        await_bytes(rows_in.at[:, pl.ds(2 * n, 2)], zo_r.at[n])
        from_planes(n)
        store(n).start()

    def store(n):
        bands = pl.ds(2 * n, 2)
        return pltpu.make_async_copy(xout.at[:, bands], out.at[:, bands], st_s.at[n])

    def gram_fields(q):
        await_bytes(xp.at[pl.ds(PART * q, PART)], xp_r.at[q])
        x = [192 * h + 12 * b + PART * q + i for i in range(PART)]
        gram(xp, q, [vxy[pl.ds(i, 1), :] for i in x])

    gram_fields(0)
    gram_fields(1)
    gram_fields(2)
    gram_fields(3)

    gb[...] = gt[...].astype(BF)

    def sb_send(target):
        remote(
            gb.at[at(target, 16, 16), :], sb.at[b], sb_s.at[0], sb_r.at[0], target, g
        ).start()

    each(1, 16, lambda k: sb_send(band_peer(k)))
    local(gb.at[at(b, 16, 16), :], sb.at[b], sb_r.at[0])
    await_bytes(p2.at[pl.ds(0, 180)], xp_s.at[0])
    each(0, 2, finish)
    await_bytes(sb, sb_r.at[0])
    total = sb[0].astype(F32)
    for k in range(1, 16):
        total = total + sb[k].astype(F32)
    st[...] = jnp.concatenate([total, jnp.zeros((112, 256), F32)], axis=0).T

    def sa_send(target):
        remote(
            st.at[at(target, 32, 8), :], sa.at[g], sa_s.at[0], sa_r.at[0], b, target
        ).start()

    each(1, 8, lambda k: sa_send(ga_peer(k)))
    local(st.at[at(g, 32, 8), :], sa.at[g], sa_r.at[0])
    each(2, 4, finish)
    await_bytes(w1.at[:, pl.ds(0, 7)], zo_s.at[0])
    await_bytes(sb.at[pl.ds(0, 15)], sb_s.at[0])
    await_bytes(sa, sa_r.at[0])
    block = sa[0]
    for k in range(1, 8):
        block = block + sa[k]
    block = jnp.concatenate([block, jnp.zeros((96, 128), F32)], axis=0).T[0:16]
    row = lax.broadcasted_iota(jnp.int32, (128, 128), 0)
    col = lax.broadcasted_iota(jnp.int32, (128, 128), 1)
    lane = ((col >> 3) << 4) + (col & 7)
    valid = col < 16
    pick_re = jnp.where(valid & (row == lane), 1.0, 0.0)
    pick_im = jnp.where(valid & (row == lane + 8), 1.0, 0.0)

    def pick(rows, which):
        return jnp.dot(rows, which, precision=lax.Precision.HIGHEST, preferred_element_type=F32)

    inverse_cells = 1.0 / (4 * N * N)
    rr, ri = pick(block, pick_re), pick(block, pick_im)
    sub[0] = ((rr[0:8] + ri[8:16]) * inverse_cells)[:, 0:16]
    sub[1] = ((ri[0:8] - rr[8:16]) * inverse_cells)[:, 0:16]

    await_bytes(sa.at[pl.ds(0, 7)], sa_s.at[0])
    each(0, 4, lambda n: store(n).wait())


def finished(rows, sums, out, sub):
    out[...] = rows[...]
    sub[...] = sums[...]


def shards(table, waves, ionic_field, point_charge, charge_place, charge_slab):
    tiled = waves.reshape(2, 8, 4, 144, 128).transpose(0, 1, 3, 2, 4).reshape(2, 8, 36, 16, 128)
    dma = pltpu.SemaphoreType.DMA
    vmem = pltpu.VMEM
    hbm = pl.BlockSpec(memory_space=pltpu.MemorySpace.HBM)
    out, sub = pl.pallas_call(
        kernel,
        out_shape=(
            jax.ShapeDtypeStruct((2, 8, 36, 16, 128), BF),
            jax.ShapeDtypeStruct((2, 8, 16), F32),
        ),
        in_specs=[hbm] + [pl.BlockSpec(memory_space=pltpu.VMEM)] * 4 + [hbm],
        out_specs=(
            hbm,
            pl.BlockSpec(memory_space=pltpu.VMEM),
        ),
        scratch_shapes=[
            vmem((2, 8, 36, 16, 128), BF),
            vmem((2, 8, 4, ROWS, N), BF),
            vmem((2, N, N), F32),
            vmem((2, 8, 4, ROWS, N), BF),
            vmem((2, 8, 36, 16, 128), BF),
            vmem((192, 192), BF),
            vmem((192, 192), BF),
            vmem((2 * N, 2 * N), BF),
            vmem((2 * N, 2 * N), BF),
            vmem((256, 256), BF),
            vmem((N, N), F32),
            vmem((2, 4, N, N), BF),
            vmem((192, 16, N), BF),
            vmem((12, 256, N), BF),
            vmem((4, 2, N, N), BF),
            vmem((4, 2, N, N), F32),
            vmem((2, 8, 192, N), BF),
            vmem((192, 16, N), BF),
            vmem((12, 256, N), BF),
            vmem((2, 4, N, N), BF),
            vmem((2 * N, N), BF),
            vmem((2 * N, N), BF),
            vmem((N, 2 * N), BF),
            vmem((8, 256), F32),
            vmem((8, 8, 256), F32),
            vmem((4, 16, N), F32),
            vmem((16, N), F32),
            vmem((256, N), F32),
            vmem((16, 16, N), F32),
            vmem((16, N), BF),
            vmem((2, 256, N), BF),
            vmem((N, N), F32),
            vmem((N, N), F32),
            vmem((256, 256), F32),
            vmem((256, 256), BF),
            vmem((8, 32, 128), F32),
            vmem((256, 128), F32),
            vmem((16, 16, 256), BF),
            dma((1,)), dma((4,)),
            dma((1,)), dma((4,)),
            dma((1,)), dma((1,)),
            dma((4,)), dma((1,)),
            dma((1,)), dma((1,)),
            dma((1,)), dma((1,)),
            dma((1,)), dma((1,)),
            dma((1,)), dma((4,)),
            dma((1,)), dma((PARTS,)),
            dma((1,)), dma((PARTS,)),
            dma((1,)), dma((1,)),
            dma((1,)), dma((1,)),
            dma((5,)),
            dma((4,)),
        ],
        compiler_params=pltpu.CompilerParams(
            collective_id=0, has_side_effects=True, vmem_limit_bytes=56 * 1024 * 1024
        ),
    )(
        tiled, point_charge.reshape(1, 256), charge_place, charge_slab.reshape(1, 256),
        ionic_field, table,
    )
    halves = pl.BlockSpec((2, 4, 36, 16, 128), lambda i: (0, i, 0, 0, 0))
    every = pl.BlockSpec((2, 8, 16), lambda i: (0, 0, 0))
    out, sub = pl.pallas_call(
        finished,
        out_shape=(
            jax.ShapeDtypeStruct((2, 8, 36, 16, 128), BF),
            jax.ShapeDtypeStruct((2, 8, 16), F32),
        ),
        grid=(2,),
        in_specs=[halves, every],
        out_specs=(halves, every),
    )(out, sub)
    out = out.reshape(2, 8, 144, 4, 128).transpose(0, 1, 3, 2, 4)
    return out.reshape(2, 8, 4, ROWS * N), sub


def solution(mesh):
    placed = (
        P(None, "band", None, "ga"),
        P("ga", None),
        P(("band", "ga")),
        P(None, ("band", "ga")),
        P(("band", "ga"), None),
    )
    mapped = jax.shard_map(
        shards,
        mesh=mesh,
        in_specs=(P(None, None, None),) + placed,
        out_specs=(P(None, "band", None, "ga"), P(None, "band", "ga")),
        check_vma=False,
    )
    return functools.partial(mapped, tables())
```

```python
import functools

import jax
import jax.numpy as jnp
import ml_dtypes
import numpy as np
from jax import lax
from jax.experimental import pallas as pl
from jax.experimental.pallas import tpu as pltpu
from jax.sharding import PartitionSpec as P

N = 384
ROWS = 48
BF = jnp.bfloat16
F32 = jnp.float32
MESH = pl.DeviceIdType.MESH


def tables():
    indices = np.arange(N, dtype=np.int32)
    phases = indices[:, None] * indices[None, :] % N
    angles = phases.astype(np.float32) * np.float32(2.0 * np.pi / N)
    factor = np.float32(1.0) / np.sqrt(np.float32(N))
    both = np.stack([np.cos(angles) * factor, np.sin(angles) * factor])
    return both.astype(ml_dtypes.bfloat16).astype(np.float32)


def dot(a, b):
    return jnp.dot(a, b, preferred_element_type=F32)


def dot_nt(a, b):
    return lax.dot_general(a, b, (((1,), (1,)), ((), ())), preferred_element_type=F32)


def split(value):
    high = value.astype(BF)
    return high, (value - high.astype(F32)).astype(BF)


def gaussian(distance):
    return jnp.exp(-distance * distance / 4.5)


SHIFTS = (
    (0, 1), (1, 0), (0, 3), (3, 0), (2, 2), (1, 1), (3, 3), (1, 3),
    (3, 1), (0, 2), (2, 0), (1, 2), (2, 1), (3, 2), (2, 3),
)
PARTS = 4
PART = 12 // PARTS


def each(low, high, body):
    def step(k, c):
        body(k)
        return c

    lax.fori_loop(low, high, step, 0)


def at(start, size, step):
    return pl.ds(pl.multiple_of(start * size, step), size)


def place_of(row):
    m = row >> 4
    plane = (m * 11) >> 5
    return ((row & 15) * 3 + m - 3 * plane) * 4 + plane


def kernel(
    waves, charge, place, slab_in, ionic, tab_in, out, sub,
    xin, w1, tab, rows_in, spread, gather, m1, m2, perm, kin, zb, w2, xw, phi, wide, ph, p2, xp, ab, fs, ts, bs,
    chs, ch, ios, iop, pot, rsb, own, pf, vyx, vxy, gt, gb, sa, st, sb,
    zi_s, zi_r, zo_s, zo_r, ch_s, ch_r, io_s, io_r, rs_s, rs_r, ag_s, ag_r,
    sp_s, sp_r, sf_s, sf_r, xw_s, xw_r, xp_s, xp_r, sa_s, sa_r, sb_s, sb_r, loc,
):
    b = lax.axis_index("band")
    g = lax.axis_index("ga")
    z = g // 2
    h = lax.rem(g, 2)
    sibling = g + 1 - 2 * h
    b_y = b // 4
    b_x = lax.rem(b, 4)

    def ga_peer(k):
        return lax.rem(g + k, 8)

    def band_peer(k):
        return lax.rem(b + k, 16)

    def shifted(dy, dx):
        return lax.rem(b_y + dy, 4) * 4 + lax.rem(b_x + dx, 4)

    def remote(src, dst, send, recv, band, ga):
        return pltpu.make_async_remote_copy(
            src_ref=src, dst_ref=dst, send_sem=send, recv_sem=recv,
            device_id=(band, ga), device_id_type=MESH,
        )

    barrier = pltpu.get_barrier_semaphore()
    each(1, 8, lambda k: pl.semaphore_signal(
        barrier, inc=1, device_id=(b, ga_peer(k)), device_id_type=MESH))
    each(1, 16, lambda k: pl.semaphore_signal(
        barrier, inc=1, device_id=(band_peer(k), g), device_id_type=MESH))

    def load(n):
        return pltpu.make_async_copy(
            waves.at[:, pl.ds(2 * n, 2)], xin.at[:, pl.ds(2 * n, 2)], loc.at[n]
        )

    def load_tab():
        return pltpu.make_async_copy(tab_in, tab, loc.at[4])

    for n in range(4):
        load(n).start()
    load_tab().start()

    lead = lax.broadcasted_iota(jnp.int32, (192, 192), 0)
    last = lax.broadcasted_iota(jnp.int32, (192, 192), 1)
    spread[...] = jnp.where(last == place_of(lead), 1.0, 0.0).astype(BF)
    gather[...] = jnp.where(lead == place_of(last), 1.0, 0.0).astype(BF)

    def to_planes(n):
        load(n).wait()
        for core in range(2):
            for x in range(3):
                both = jnp.concatenate(
                    [xin[c, 2 * n + core, 12 * x : 12 * x + 12].reshape(192, 128) for c in range(2)],
                    axis=1,
                )
                rows = dot(spread[...], both).astype(BF)
                for m in range(12):
                    part = m % 3 * 128
                    for c in range(2):
                        w1[c, 2 * n + core, m // 3, 16 * x : 16 * x + 16, part : part + 128] = (
                            rows[16 * m : 16 * m + 16, 128 * c : 128 * c + 128]
                        )

    def from_planes(n):
        for core in range(2):
            for x in range(3):
                both = jnp.concatenate(
                    [
                        jnp.concatenate(
                            [
                                rows_in[
                                    c, 2 * n + core, m // 3, 16 * x : 16 * x + 16,
                                    m % 3 * 128 : m % 3 * 128 + 128,
                                ]
                                for m in range(12)
                            ],
                            axis=0,
                        )
                        for c in range(2)
                    ],
                    axis=1,
                )
                rows = dot(gather[...], both).astype(BF)
                for c in range(2):
                    out[c, 2 * n + core, 12 * x : 12 * x + 12] = rows[
                        :, 128 * c : 128 * c + 128
                    ].reshape(12, 16, 128)

    chs[0:1] = charge[...]
    chs[1:4] = place[...]
    chs[4:5] = slab_in[...].astype(F32)
    chs[5:8] = jnp.zeros((3, 256), F32)
    each(0, 4, to_planes)

    to = lax.broadcasted_iota(jnp.int32, (256, 256), 0)
    of = lax.broadcasted_iota(jnp.int32, (256, 256), 1)
    perm[...] = jnp.where(
        ((to >> 4) == (of & 15)) & ((to & 15) == (of >> 4)), 1.0, 0.0
    ).astype(BF)
    def turn(p):
        for x in range(3):
            block = w1[:, :, p, 16 * x : 16 * x + 16, :].reshape(256, N)
            turned = dot(perm[...], block).astype(BF).reshape(16, 16, N)
            w2[pl.ds(ROWS * p + 16 * x, 16)] = turned

    each(0, 4, turn)
    pl.semaphore_wait(barrier, 22)

    def local(src, dst, sem):
        pltpu.make_async_copy(src, dst, sem).start()

    def await_bytes(like, sem):
        pltpu.make_async_copy(like, like, sem).wait()

    def ch_send(target):
        remote(chs, ch.at[g], ch_s.at[0], ch_r.at[0], b, target).start()

    io_sends = lax.rem(g, 4) == b_y
    io_half = g // 4
    io_source = 4 * h + b_y

    def io_copy(plane):
        return remote(
            ios.at[plane], iop, io_s.at[plane], io_r.at[0], b, 2 * plane + io_half
        )

    def zi_send(n, target):
        remote(
            w1.at[:, 2 * n + lax.rem(target, 2), target // 2],
            zb.at[:, n, at(g, ROWS, 16), :], zi_s.at[0], zi_r.at[n], b, target,
        ).start()

    def zo_send(n, target):
        remote(
            ab.at[:, n, at(target, ROWS, 16), :],
            rows_in.at[:, 2 * n + h, z], zo_s.at[0], zo_r.at[n], b, target,
        ).start()

    def row_sends(q, src, dst, send, recv):
        def to(target):
            return src.at[pl.ds(ROWS * q + PART * target, PART)], dst.at[pl.ds(PART * q, PART), at(b, 16, 16), :]

        for dy, dx in SHIFTS:
            target = shifted(dy, dx)
            one, other = to(target)
            remote(one, other, send.at[0], recv.at[q], target, g).start()
        one, other = to(b)
        local(one, other, recv.at[q])

    def sp_copy(half):
        return remote(pf.at[half], pf.at[half], sp_s.at[0], sp_r.at[0], b, sibling)

    def sf_copy(n, core):
        return remote(
            phi.at[n, :, at(1 - core, 192, 16), :], ph.at[:, 2 * n + core],
            sf_s.at[0], sf_r.at[n], b, sibling,
        )

    each(1, 8, lambda k: ch_send(ga_peer(k)))
    local(chs, ch.at[g], ch_r.at[0])
    def zi_all(n):
        each(1, 8, lambda k: zi_send(n, ga_peer(k)))
        local(w1.at[:, 2 * n + h, z], zb.at[:, n, at(g, ROWS, 16), :], zi_r.at[n])

    zi_all(0)

    def send_waves(q):
        row_sends(q, w2, xw, xw_s, xw_r)

    send_waves(0)
    send_waves(1)
    each(1, 4, zi_all)

    @pl.when(io_sends)
    def _():
        for j in range(4):
            @pl.when(b_x == j)
            def _(j=j):
                for plane in range(4):
                    rows = ionic[12 * j : 12 * j + 12, plane * N : (plane + 1) * N]
                    ios[plane] = jnp.concatenate([rows, jnp.zeros((4, N), F32)], axis=0)
        for plane in range(4):
            @pl.when(2 * plane + io_half != g)
            def _(plane=plane):
                io_copy(plane).start()

    load_tab().wait()
    c = tab[0].astype(BF)
    s = tab[1].astype(BF)
    m1[0:N, 0:N] = c
    m1[0:N, N : 2 * N] = s
    m1[N : 2 * N, 0:N] = -s
    m1[N : 2 * N, N : 2 * N] = c
    m2[0:N, 0:N] = c
    m2[0:N, N : 2 * N] = -s
    m2[N : 2 * N, 0:N] = s
    m2[N : 2 * N, N : 2 * N] = c

    def frequency(indices):
        return jnp.where(indices < N // 2, indices, indices - N).astype(F32)

    fx = frequency(lax.broadcasted_iota(jnp.int32, (N, N), 0))
    fy = frequency(lax.broadcasted_iota(jnp.int32, (N, N), 1))
    kin[...] = 2.0 * (fx * fx / (N * N) + fy * fy / (N * N))

    await_bytes(ch, ch_r.at[0])
    pot[...] = jnp.zeros((256, N), F32)

    def add_charges(source):
        rows = ch[source]
        q, u, v, w, slab = (rows[i : i + 1] for i in range(5))
        r = lax.broadcasted_iota(jnp.int32, (256, 256), 0)
        y = 192 * h + 12 * (r >> 4) + (r & 15)
        weight = q * gaussian(z.astype(F32) - 4.0 * w)
        inside = ((y * 1366) >> 16).astype(F32) == slab
        gy = gaussian(y.astype(F32) - (slab * 48.0 + 48.0 * v)) * weight
        gy = jnp.where(inside, gy, 0.0)
        x = lax.broadcasted_iota(jnp.int32, (N, 256), 0).astype(F32)
        gx = gaussian(x - 384.0 * u)
        yh, yl = split(gy)
        xh, xl = split(gx)
        pot[...] += dot_nt(yh, xh) + (dot_nt(yh, xl) + dot_nt(yl, xh))

    def add_two(i):
        add_charges(2 * i)
        add_charges(2 * i + 1)

    each(0, 4, add_two)

    def rs_send(target):
        remote(
            pot.at[at(target, 16, 8), :], rsb.at[b], rs_s.at[0], rs_r.at[0], target, g
        ).start()

    each(1, 16, lambda k: rs_send(band_peer(k)))
    local(pot.at[at(b, 16, 8), :], rsb.at[b], rs_r.at[0])
    send_waves(2)

    def forward(n):
        await_bytes(zb.at[:, n], zi_r.at[n])
        both = jnp.concatenate([zb[0, n], zb[1, n]], axis=1)
        fs[0:N] = dot(both, m1[:, 0:N]).astype(BF)
        fs[N : 2 * N] = dot(both, m1[:, N : 2 * N]).astype(BF)
        for part in range(2):
            space = dot(m2[part * N : (part + 1) * N], fs[...])
            wide[n, part] = space
            phi[n, part] = space.astype(BF)
        sf_copy(n, h).start()
        for part in range(2):
            ph[part, 2 * n + h] = phi[n, part, at(h, 192, 16), :]

    each(0, 2, forward)

    await_bytes(rsb, rs_r.at[0])

    @pl.when(io_source == g)
    def _():
        iop[...] = ios[z]

    @pl.when(io_source != g)
    def _():
        io_copy(z).wait_recv()

    piece = iop[...]
    for k in range(16):
        piece = piece + rsb[k]
    own[...] = piece.astype(BF)

    def ag_send(target):
        remote(own, pf.at[h, at(b, 16, 16), :], ag_s.at[0], ag_r.at[0], target, g).start()

    each(1, 16, lambda k: ag_send(band_peer(k)))
    local(own, pf.at[h, at(b, 16, 16), :], ag_r.at[0])
    send_waves(3)
    each(2, 4, forward)
    await_bytes(pf.at[h], ag_r.at[0])
    sp_copy(h).start()

    each(0, 4, lambda n: sf_copy(n, 1 - h).wait_recv())

    def turn_field(p):
        for x in range(3):
            block = ph[:, :, at(3 * p + x, 16, 16), :].reshape(256, N)
            p2[at(3 * p + x, 16, 16)] = dot(perm[...], block).astype(BF).reshape(16, 16, N)

    for q in range(PARTS):
        turn_field(q)
        row_sends(q, p2, xp, xp_s, xp_r)

    sp_copy(1 - h).wait_recv()
    for half in range(2):
        def join(q, half=half):
            two = pf[half, at(q, 32, 16), :].astype(F32)
            dst = pl.ds(pl.multiple_of(192 * half + 24 * q, 8), 24)
            vyx[dst, :] = jnp.concatenate([two[0:12], two[16:28]], axis=0)

        each(0, 8, join)
    vxy[...] = vyx[...].T

    def backward(n):
        for part in range(2):
            ts[part * N : (part + 1) * N] = (wide[n, part] * vxy[...]).astype(BF)
        for part in range(2):
            bs[:, part * N : (part + 1) * N] = dot(
                m1[part * N : (part + 1) * N], ts[...]
            ).astype(BF)
        for part in range(2):
            recip = dot(bs[...], m2[:, part * N : (part + 1) * N])
            ab[part, n] = (kin[...] * zb[part, n].astype(F32) + recip).astype(BF)
        each(1, 8, lambda k: zo_send(n, ga_peer(k)))
        local(ab.at[:, n, at(g, ROWS, 16), :], rows_in.at[:, 2 * n + h, z], zo_r.at[n])

    each(0, 4, backward)

    def gram(data, q, weights):
        rows = [data[PART * q + i] for i in range(PART)]
        scaled = [(r.astype(F32) * w).astype(BF) for r, w in zip(rows, weights)]
        gt[...] += dot_nt(jnp.concatenate(rows, axis=1), jnp.concatenate(scaled, axis=1))

    gt[...] = jnp.zeros((256, 256), F32)

    def gram_waves(q):
        await_bytes(xw.at[pl.ds(PART * q, PART)], xw_r.at[q])
        x = [ROWS * g + PART * b + i for i in range(PART)]
        gram(xw, q, [kin[pl.ds(i, 1), :] for i in x])

    each(0, PARTS, gram_waves)

    await_bytes(w1.at[:, pl.ds(0, 7)], zi_s.at[0])
    await_bytes(ph.at[:, pl.ds(0, 4)], sf_s.at[0])
    await_bytes(ch.at[pl.ds(0, 7)], ch_s.at[0])
    await_bytes(rsb.at[pl.ds(0, 15)], rs_s.at[0])
    await_bytes(pf.at[0, pl.ds(0, 240)], ag_s.at[0])
    await_bytes(w2.at[pl.ds(0, 180)], xw_s.at[0])
    sp_copy(h).wait_send()

    @pl.when(io_sends)
    def _():
        for plane in range(4):
            @pl.when(2 * plane + io_half != g)
            def _(plane=plane):
                io_copy(plane).wait_send()

    def finish(n):
        await_bytes(rows_in.at[:, pl.ds(2 * n, 2)], zo_r.at[n])
        from_planes(n)

    def gram_fields(q):
        await_bytes(xp.at[pl.ds(PART * q, PART)], xp_r.at[q])
        x = [192 * h + ROWS * q + PART * b + i for i in range(PART)]
        gram(xp, q, [vxy[pl.ds(i, 1), :] for i in x])

    gram_fields(0)
    gram_fields(1)
    gram_fields(2)
    each(0, 2, finish)
    gram_fields(3)

    gb[...] = gt[...].astype(BF)

    def sb_send(target):
        remote(
            gb.at[at(target, 16, 16), :], sb.at[b], sb_s.at[0], sb_r.at[0], target, g
        ).start()

    each(1, 16, lambda k: sb_send(band_peer(k)))
    local(gb.at[at(b, 16, 16), :], sb.at[b], sb_r.at[0])
    await_bytes(p2.at[pl.ds(0, 180)], xp_s.at[0])
    finish(2)
    await_bytes(sb, sb_r.at[0])
    total = sb[0].astype(F32)
    for k in range(1, 16):
        total = total + sb[k].astype(F32)
    st[...] = jnp.concatenate([total, jnp.zeros((112, 256), F32)], axis=0).T

    def sa_send(target):
        remote(
            st.at[at(target, 32, 8), :], sa.at[g], sa_s.at[0], sa_r.at[0], b, target
        ).start()

    each(1, 8, lambda k: sa_send(ga_peer(k)))
    local(st.at[at(g, 32, 8), :], sa.at[g], sa_r.at[0])
    finish(3)
    await_bytes(w1.at[:, pl.ds(0, 7)], zo_s.at[0])
    await_bytes(sb.at[pl.ds(0, 15)], sb_s.at[0])
    await_bytes(sa, sa_r.at[0])
    block = sa[0]
    for k in range(1, 8):
        block = block + sa[k]
    block = jnp.concatenate([block, jnp.zeros((96, 128), F32)], axis=0).T[0:16]
    row = lax.broadcasted_iota(jnp.int32, (128, 128), 0)
    col = lax.broadcasted_iota(jnp.int32, (128, 128), 1)
    lane = ((col >> 3) << 4) + (col & 7)
    valid = col < 16
    pick_re = jnp.where(valid & (row == lane), 1.0, 0.0)
    pick_im = jnp.where(valid & (row == lane + 8), 1.0, 0.0)

    def pick(rows, which):
        return jnp.dot(rows, which, precision=lax.Precision.HIGHEST, preferred_element_type=F32)

    inverse_cells = 1.0 / (4 * N * N)
    rr, ri = pick(block, pick_re), pick(block, pick_im)
    sub[0] = ((rr[0:8] + ri[8:16]) * inverse_cells)[:, 0:16]
    sub[1] = ((ri[0:8] - rr[8:16]) * inverse_cells)[:, 0:16]

    await_bytes(sa.at[pl.ds(0, 7)], sa_s.at[0])


def shards(table, waves, ionic_field, point_charge, charge_place, charge_slab):
    tiled = waves.reshape(2, 8, 4, 144, 128).transpose(0, 1, 3, 2, 4).reshape(2, 8, 36, 16, 128)
    dma = pltpu.SemaphoreType.DMA
    vmem = pltpu.VMEM
    hbm = pl.BlockSpec(memory_space=pltpu.MemorySpace.HBM)
    out, sub = pl.pallas_call(
        kernel,
        out_shape=(
            vmem((2, 8, 36, 16, 128), BF),
            vmem((2, 8, 16), F32),
        ),
        in_specs=[hbm] + [pl.BlockSpec(memory_space=pltpu.VMEM)] * 4 + [hbm],
        out_specs=(
            pl.BlockSpec(memory_space=pltpu.VMEM),
            pl.BlockSpec(memory_space=pltpu.VMEM),
        ),
        scratch_shapes=[
            vmem((2, 8, 36, 16, 128), BF),
            vmem((2, 8, 4, ROWS, N), BF),
            vmem((2, N, N), F32),
            vmem((2, 8, 4, ROWS, N), BF),
            vmem((192, 192), BF),
            vmem((192, 192), BF),
            vmem((2 * N, 2 * N), BF),
            vmem((2 * N, 2 * N), BF),
            vmem((256, 256), BF),
            vmem((N, N), F32),
            vmem((2, 4, N, N), BF),
            vmem((192, 16, N), BF),
            vmem((12, 256, N), BF),
            vmem((4, 2, N, N), BF),
            vmem((4, 2, N, N), F32),
            vmem((2, 8, 192, N), BF),
            vmem((192, 16, N), BF),
            vmem((12, 256, N), BF),
            vmem((2, 4, N, N), BF),
            vmem((2 * N, N), BF),
            vmem((2 * N, N), BF),
            vmem((N, 2 * N), BF),
            vmem((8, 256), F32),
            vmem((8, 8, 256), F32),
            vmem((4, 16, N), F32),
            vmem((16, N), F32),
            vmem((256, N), F32),
            vmem((16, 16, N), F32),
            vmem((16, N), BF),
            vmem((2, 256, N), BF),
            vmem((N, N), F32),
            vmem((N, N), F32),
            vmem((256, 256), F32),
            vmem((256, 256), BF),
            vmem((8, 32, 128), F32),
            vmem((256, 128), F32),
            vmem((16, 16, 256), BF),
            dma((1,)), dma((4,)),
            dma((1,)), dma((4,)),
            dma((1,)), dma((1,)),
            dma((4,)), dma((1,)),
            dma((1,)), dma((1,)),
            dma((1,)), dma((1,)),
            dma((1,)), dma((1,)),
            dma((1,)), dma((4,)),
            dma((1,)), dma((PARTS,)),
            dma((1,)), dma((PARTS,)),
            dma((1,)), dma((1,)),
            dma((1,)), dma((1,)),
            dma((5,)),
        ],
        compiler_params=pltpu.CompilerParams(
            collective_id=0, has_side_effects=True, vmem_limit_bytes=56 * 1024 * 1024
        ),
    )(
        tiled, point_charge.reshape(1, 256), charge_place, charge_slab.reshape(1, 256),
        ionic_field, table,
    )
    out = out.reshape(2, 8, 144, 4, 128).transpose(0, 1, 3, 2, 4)
    return out.reshape(2, 8, 4, ROWS * N), sub


def solution(mesh):
    placed = (
        P(None, "band", None, "ga"),
        P("ga", None),
        P(("band", "ga")),
        P(None, ("band", "ga")),
        P(("band", "ga"), None),
    )
    mapped = jax.shard_map(
        shards,
        mesh=mesh,
        in_specs=(P(None, None, None),) + placed,
        out_specs=(P(None, "band", None, "ga"), P(None, "band", "ga")),
        check_vma=False,
    )
    return functools.partial(mapped, tables())
```

```python
import functools

import jax
import jax.numpy as jnp
import ml_dtypes
import numpy as np
from jax import lax
from jax.experimental import pallas as pl
from jax.experimental.pallas import tpu as pltpu
from jax.sharding import PartitionSpec as P

N = 384
ROWS = 48
BF = jnp.bfloat16
F32 = jnp.float32
MESH = pl.DeviceIdType.MESH


def tables():
    indices = np.arange(N, dtype=np.int32)
    phases = indices[:, None] * indices[None, :] % N
    angles = phases.astype(np.float32) * np.float32(2.0 * np.pi / N)
    factor = np.float32(1.0) / np.sqrt(np.float32(N))
    both = np.stack([np.cos(angles) * factor, np.sin(angles) * factor])
    return both.astype(ml_dtypes.bfloat16).astype(np.float32)


def dot(a, b):
    return jnp.dot(a, b, preferred_element_type=F32)


def dot_nt(a, b):
    return lax.dot_general(a, b, (((1,), (1,)), ((), ())), preferred_element_type=F32)


def split(value):
    high = value.astype(BF)
    return high, (value - high.astype(F32)).astype(BF)


def gaussian(distance):
    return jnp.exp(-distance * distance / 4.5)


SHIFTS = (
    (0, 1), (1, 0), (0, 3), (3, 0), (2, 2), (1, 1), (3, 3), (1, 3),
    (3, 1), (0, 2), (2, 0), (1, 2), (2, 1), (3, 2), (2, 3),
)
PARTS = 4
PART = 12 // PARTS


def each(low, high, body):
    def step(k, c):
        body(k)
        return c

    lax.fori_loop(low, high, step, 0)


def at(start, size, step):
    return pl.ds(pl.multiple_of(start * size, step), size)


def place_of(row):
    m = row >> 4
    plane = (m * 11) >> 5
    return ((row & 15) * 3 + m - 3 * plane) * 4 + plane


def kernel(
    waves, charge, place, slab_in, ionic, tab_in, out, sub,
    xin, w1, tab, rows_in, spread, gather, m1, m2, perm, kin, zb, w2, xw, phi, wide, ph, p2, xp, ab, fs, ts, bs,
    chs, ch, ios, iop, pot, pt, rsb, own, pf, vyx, vxy, gt, gb, sa, st, sb,
    zi_s, zi_r, zo_s, zo_r, ch_s, ch_r, io_s, io_r, rs_s, rs_r, ag_s, ag_r,
    sp_s, sp_r, sf_s, sf_r, xw_s, xw_r, xp_s, xp_r, sa_s, sa_r, sb_s, sb_r, loc,
):
    b = lax.axis_index("band")
    g = lax.axis_index("ga")
    z = g // 2
    h = lax.rem(g, 2)
    sibling = g + 1 - 2 * h
    b_y = b // 4
    b_x = lax.rem(b, 4)

    def ga_peer(k):
        return lax.rem(g + k, 8)

    def band_peer(k):
        return lax.rem(b + k, 16)

    def shifted(dy, dx):
        return lax.rem(b_y + dy, 4) * 4 + lax.rem(b_x + dx, 4)

    def remote(src, dst, send, recv, band, ga):
        return pltpu.make_async_remote_copy(
            src_ref=src, dst_ref=dst, send_sem=send, recv_sem=recv,
            device_id=(band, ga), device_id_type=MESH,
        )

    barrier = pltpu.get_barrier_semaphore()
    each(1, 8, lambda k: pl.semaphore_signal(
        barrier, inc=1, device_id=(b, ga_peer(k)), device_id_type=MESH))
    each(1, 16, lambda k: pl.semaphore_signal(
        barrier, inc=1, device_id=(band_peer(k), g), device_id_type=MESH))

    def load(n):
        return pltpu.make_async_copy(
            waves.at[:, pl.ds(2 * n, 2)], xin.at[:, pl.ds(2 * n, 2)], loc.at[n]
        )

    def load_tab():
        return pltpu.make_async_copy(tab_in, tab, loc.at[4])

    for n in range(4):
        load(n).start()
    load_tab().start()

    lead = lax.broadcasted_iota(jnp.int32, (192, 192), 0)
    last = lax.broadcasted_iota(jnp.int32, (192, 192), 1)
    spread[...] = jnp.where(last == place_of(lead), 1.0, 0.0).astype(BF)
    gather[...] = jnp.where(lead == place_of(last), 1.0, 0.0).astype(BF)

    def to_planes(n):
        load(n).wait()
        for core in range(2):
            for x in range(3):
                both = jnp.concatenate(
                    [xin[c, 2 * n + core, 12 * x : 12 * x + 12].reshape(192, 128) for c in range(2)],
                    axis=1,
                )
                rows = dot(spread[...], both).astype(BF)
                for m in range(12):
                    part = m % 3 * 128
                    for c in range(2):
                        w1[c, 2 * n + core, m // 3, 16 * x : 16 * x + 16, part : part + 128] = (
                            rows[16 * m : 16 * m + 16, 128 * c : 128 * c + 128]
                        )

    def from_planes(n):
        for core in range(2):
            for x in range(3):
                both = jnp.concatenate(
                    [
                        jnp.concatenate(
                            [
                                rows_in[
                                    c, 2 * n + core, m // 3, 16 * x : 16 * x + 16,
                                    m % 3 * 128 : m % 3 * 128 + 128,
                                ]
                                for m in range(12)
                            ],
                            axis=0,
                        )
                        for c in range(2)
                    ],
                    axis=1,
                )
                rows = dot(gather[...], both).astype(BF)
                for c in range(2):
                    out[c, 2 * n + core, 12 * x : 12 * x + 12] = rows[
                        :, 128 * c : 128 * c + 128
                    ].reshape(12, 16, 128)

    chs[0:1] = charge[...]
    chs[1:4] = place[...]
    chs[4:5] = slab_in[...].astype(F32)
    chs[5:8] = jnp.zeros((3, 256), F32)
    each(0, 4, to_planes)

    to = lax.broadcasted_iota(jnp.int32, (256, 256), 0)
    of = lax.broadcasted_iota(jnp.int32, (256, 256), 1)
    perm[...] = jnp.where(
        ((to >> 4) == (of & 15)) & ((to & 15) == (of >> 4)), 1.0, 0.0
    ).astype(BF)
    def turn(p):
        for x in range(3):
            block = w1[:, :, p, 16 * x : 16 * x + 16, :].reshape(256, N)
            turned = dot(perm[...], block).astype(BF).reshape(16, 16, N)
            w2[pl.ds(ROWS * p + 16 * x, 16)] = turned

    each(0, 4, turn)
    pl.semaphore_wait(barrier, 22)

    def local(src, dst, sem):
        pltpu.make_async_copy(src, dst, sem).start()

    def await_bytes(like, sem):
        pltpu.make_async_copy(like, like, sem).wait()

    def ch_send(target):
        remote(chs, ch.at[g], ch_s.at[0], ch_r.at[0], b, target).start()

    io_sends = lax.rem(g, 4) == b_y
    io_half = g // 4
    io_source = 4 * h + b_y

    def io_copy(plane):
        return remote(
            ios.at[plane], iop, io_s.at[plane], io_r.at[0], b, 2 * plane + io_half
        )

    def zi_send(n, target):
        remote(
            w1.at[:, 2 * n + lax.rem(target, 2), target // 2],
            zb.at[:, n, at(g, ROWS, 16), :], zi_s.at[0], zi_r.at[n], b, target,
        ).start()

    def zo_send(n, target):
        remote(
            ab.at[:, n, at(target, ROWS, 16), :],
            rows_in.at[:, 2 * n + h, z], zo_s.at[0], zo_r.at[n], b, target,
        ).start()

    def row_sends(q, src, dst, send, recv):
        def to(target):
            return src.at[pl.ds(ROWS * q + PART * target, PART)], dst.at[pl.ds(PART * q, PART), at(b, 16, 16), :]

        for dy, dx in SHIFTS:
            target = shifted(dy + h * (dx - dy), dx + h * (dy - dx))
            one, other = to(target)
            remote(one, other, send.at[0], recv.at[q], target, g).start()
        one, other = to(b)
        local(one, other, recv.at[q])

    def sp_copy(half):
        return remote(pf.at[half], pf.at[half], sp_s.at[0], sp_r.at[0], b, sibling)

    def sf_copy(n, part, core):
        return remote(
            phi.at[n, part, at(1 - core, 192, 16), :], ph.at[part, 2 * n + core],
            sf_s.at[0], sf_r.at[n], b, sibling,
        )

    each(1, 8, lambda k: ch_send(ga_peer(k)))
    local(chs, ch.at[g], ch_r.at[0])
    def zi_all(n):
        each(1, 8, lambda k: zi_send(n, ga_peer(k)))
        local(w1.at[:, 2 * n + h, z], zb.at[:, n, at(g, ROWS, 16), :], zi_r.at[n])

    zi_all(0)

    def send_waves(q):
        row_sends(q, w2, xw, xw_s, xw_r)

    send_waves(0)
    send_waves(1)
    each(1, 4, zi_all)

    @pl.when(io_sends)
    def _():
        for j in range(4):
            @pl.when(b_x == j)
            def _(j=j):
                for plane in range(4):
                    rows = ionic[12 * j : 12 * j + 12, plane * N : (plane + 1) * N]
                    ios[plane] = jnp.concatenate([rows, jnp.zeros((4, N), F32)], axis=0)
        for plane in range(4):
            @pl.when(2 * plane + io_half != g)
            def _(plane=plane):
                io_copy(plane).start()

    load_tab().wait()
    c = tab[0].astype(BF)
    s = tab[1].astype(BF)
    m1[0:N, 0:N] = c
    m1[0:N, N : 2 * N] = s
    m1[N : 2 * N, 0:N] = -s
    m1[N : 2 * N, N : 2 * N] = c
    m2[0:N, 0:N] = c
    m2[0:N, N : 2 * N] = -s
    m2[N : 2 * N, 0:N] = s
    m2[N : 2 * N, N : 2 * N] = c

    def frequency(indices):
        return jnp.where(indices < N // 2, indices, indices - N).astype(F32)

    fx = frequency(lax.broadcasted_iota(jnp.int32, (N, N), 0))
    fy = frequency(lax.broadcasted_iota(jnp.int32, (N, N), 1))
    kin[...] = 2.0 * (fx * fx / (N * N) + fy * fy / (N * N))

    await_bytes(ch, ch_r.at[0])
    pot[...] = jnp.zeros((256, N), F32)

    def add_charges(source):
        rows = ch[source]
        q, u, v, w, slab = (rows[i : i + 1] for i in range(5))
        r = lax.broadcasted_iota(jnp.int32, (256, 256), 0)
        y = 192 * h + 12 * (r >> 4) + (r & 15)
        weight = q * gaussian(z.astype(F32) - 4.0 * w)
        inside = ((y * 1366) >> 16).astype(F32) == slab
        gy = gaussian(y.astype(F32) - (slab * 48.0 + 48.0 * v)) * weight
        gy = jnp.where(inside, gy, 0.0)
        x = lax.broadcasted_iota(jnp.int32, (N, 256), 0).astype(F32)
        gx = gaussian(x - 384.0 * u)
        yh, yl = split(gy)
        xh, xl = split(gx)
        pot[...] += dot_nt(yh, xh) + (dot_nt(yh, xl) + dot_nt(yl, xh))

    def add_two(i):
        add_charges(2 * i)
        add_charges(2 * i + 1)

    each(0, 4, add_two)

    for j in range(16):
        pt[j] = pot[16 * j : 16 * j + 12, :]

    def rs_send(target):
        remote(
            pt.at[target], rsb.at[b], rs_s.at[0], rs_r.at[0], target, g
        ).start()

    each(1, 16, lambda k: rs_send(band_peer(k)))
    local(pt.at[b], rsb.at[b], rs_r.at[0])
    send_waves(2)

    def forward(n):
        await_bytes(zb.at[:, n], zi_r.at[n])
        both = jnp.concatenate([zb[0, n], zb[1, n]], axis=1)
        fs[0:N] = dot(both, m1[:, 0:N]).astype(BF)
        fs[N : 2 * N] = dot(both, m1[:, N : 2 * N]).astype(BF)
        for part in range(2):
            space = dot(m2[part * N : (part + 1) * N], fs[...])
            wide[n, part] = space
            phi[n, part] = space.astype(BF)
            sf_copy(n, part, h).start()
        for part in range(2):
            ph[part, 2 * n + h] = phi[n, part, at(h, 192, 16), :]

    each(0, 2, forward)

    await_bytes(rsb, rs_r.at[0])

    @pl.when(io_source == g)
    def _():
        iop[...] = ios[z]

    @pl.when(io_source != g)
    def _():
        io_copy(z).wait_recv()

    piece = iop[0:12]
    for k in range(16):
        piece = piece + rsb[k]
    own[...] = jnp.concatenate([piece, jnp.zeros((4, N), F32)], axis=0).astype(BF)

    def ag_send(target):
        remote(own, pf.at[h, at(b, 16, 16), :], ag_s.at[0], ag_r.at[0], target, g).start()

    each(1, 16, lambda k: ag_send(band_peer(k)))
    local(own, pf.at[h, at(b, 16, 16), :], ag_r.at[0])
    send_waves(3)
    each(2, 4, forward)

    each(0, 4, lambda n: await_bytes(ph.at[:, n], sf_r.at[n]))

    def turn_field(p):
        for x in range(3):
            block = ph[:, :, at(3 * p + x, 16, 16), :].reshape(256, N)
            p2[at(3 * p + x, 16, 16)] = dot(perm[...], block).astype(BF).reshape(16, 16, N)

    for q in range(PARTS):
        turn_field(q)
        row_sends(q, p2, xp, xp_s, xp_r)
        if q == 1:
            await_bytes(pf.at[h], ag_r.at[0])
            sp_copy(h).start()

    sp_copy(1 - h).wait_recv()
    for half in range(2):
        def join(q, half=half):
            two = pf[half, at(q, 32, 16), :].astype(F32)
            dst = pl.ds(pl.multiple_of(192 * half + 24 * q, 8), 24)
            vyx[dst, :] = jnp.concatenate([two[0:12], two[16:28]], axis=0)

        each(0, 8, join)
    vxy[...] = vyx[...].T

    def backward(n):
        for part in range(2):
            ts[part * N : (part + 1) * N] = (wide[n, part] * vxy[...]).astype(BF)
        for part in range(2):
            bs[:, part * N : (part + 1) * N] = dot(
                m1[part * N : (part + 1) * N], ts[...]
            ).astype(BF)
        for part in range(2):
            recip = dot(bs[...], m2[:, part * N : (part + 1) * N])
            ab[part, n] = (kin[...] * zb[part, n].astype(F32) + recip).astype(BF)
        each(1, 8, lambda k: zo_send(n, ga_peer(k)))
        local(ab.at[:, n, at(g, ROWS, 16), :], rows_in.at[:, 2 * n + h, z], zo_r.at[n])

    each(0, 4, backward)

    def gram(data, q, weights):
        rows = [data[PART * q + i] for i in range(PART)]
        scaled = [(r.astype(F32) * w).astype(BF) for r, w in zip(rows, weights)]
        gt[...] += dot_nt(jnp.concatenate(rows, axis=1), jnp.concatenate(scaled, axis=1))

    gt[...] = jnp.zeros((256, 256), F32)

    def gram_waves(q):
        await_bytes(xw.at[pl.ds(PART * q, PART)], xw_r.at[q])
        x = [ROWS * g + PART * b + i for i in range(PART)]
        gram(xw, q, [kin[pl.ds(i, 1), :] for i in x])

    each(0, PARTS, gram_waves)

    await_bytes(w1.at[:, pl.ds(0, 7)], zi_s.at[0])
    await_bytes(ph.at[:, pl.ds(0, 4)], sf_s.at[0])
    await_bytes(ch.at[pl.ds(0, 7)], ch_s.at[0])
    await_bytes(rsb.at[pl.ds(0, 15)], rs_s.at[0])
    await_bytes(pf.at[0, pl.ds(0, 240)], ag_s.at[0])
    await_bytes(w2.at[pl.ds(0, 180)], xw_s.at[0])
    sp_copy(h).wait_send()

    @pl.when(io_sends)
    def _():
        for plane in range(4):
            @pl.when(2 * plane + io_half != g)
            def _(plane=plane):
                io_copy(plane).wait_send()

    def finish(n):
        await_bytes(rows_in.at[:, pl.ds(2 * n, 2)], zo_r.at[n])
        from_planes(n)

    def gram_fields(q):
        await_bytes(xp.at[pl.ds(PART * q, PART)], xp_r.at[q])
        x = [192 * h + ROWS * q + PART * b + i for i in range(PART)]
        gram(xp, q, [vxy[pl.ds(i, 1), :] for i in x])

    gram_fields(0)
    gram_fields(1)
    gram_fields(2)
    each(0, 2, finish)
    gram_fields(3)

    gb[...] = gt[...].astype(BF)

    def sb_send(target):
        remote(
            gb.at[at(target, 16, 16), :], sb.at[b], sb_s.at[0], sb_r.at[0], target, g
        ).start()

    each(1, 16, lambda k: sb_send(band_peer(k)))
    local(gb.at[at(b, 16, 16), :], sb.at[b], sb_r.at[0])
    await_bytes(p2.at[pl.ds(0, 180)], xp_s.at[0])
    finish(2)
    await_bytes(sb, sb_r.at[0])
    total = sb[0].astype(F32)
    for k in range(1, 16):
        total = total + sb[k].astype(F32)
    st[...] = jnp.concatenate([total, jnp.zeros((112, 256), F32)], axis=0).T

    def sa_send(target):
        remote(
            st.at[at(target, 32, 8), :], sa.at[g], sa_s.at[0], sa_r.at[0], b, target
        ).start()

    each(1, 8, lambda k: sa_send(ga_peer(k)))
    local(st.at[at(g, 32, 8), :], sa.at[g], sa_r.at[0])
    finish(3)
    await_bytes(w1.at[:, pl.ds(0, 7)], zo_s.at[0])
    await_bytes(sb.at[pl.ds(0, 15)], sb_s.at[0])
    await_bytes(sa, sa_r.at[0])
    block = sa[0]
    for k in range(1, 8):
        block = block + sa[k]
    block = jnp.concatenate([block, jnp.zeros((96, 128), F32)], axis=0).T[0:16]
    row = lax.broadcasted_iota(jnp.int32, (128, 128), 0)
    col = lax.broadcasted_iota(jnp.int32, (128, 128), 1)
    lane = ((col >> 3) << 4) + (col & 7)
    valid = col < 16
    pick_re = jnp.where(valid & (row == lane), 1.0, 0.0)
    pick_im = jnp.where(valid & (row == lane + 8), 1.0, 0.0)

    def pick(rows, which):
        return jnp.dot(rows, which, precision=lax.Precision.HIGHEST, preferred_element_type=F32)

    inverse_cells = 1.0 / (4 * N * N)
    rr, ri = pick(block, pick_re), pick(block, pick_im)
    sub[0] = ((rr[0:8] + ri[8:16]) * inverse_cells)[:, 0:16]
    sub[1] = ((ri[0:8] - rr[8:16]) * inverse_cells)[:, 0:16]

    await_bytes(sa.at[pl.ds(0, 7)], sa_s.at[0])


def shards(table, waves, ionic_field, point_charge, charge_place, charge_slab):
    tiled = waves.reshape(2, 8, 4, 144, 128).transpose(0, 1, 3, 2, 4).reshape(2, 8, 36, 16, 128)
    dma = pltpu.SemaphoreType.DMA
    vmem = pltpu.VMEM
    hbm = pl.BlockSpec(memory_space=pltpu.MemorySpace.HBM)
    out, sub = pl.pallas_call(
        kernel,
        out_shape=(
            vmem((2, 8, 36, 16, 128), BF),
            vmem((2, 8, 16), F32),
        ),
        in_specs=[hbm] + [pl.BlockSpec(memory_space=pltpu.VMEM)] * 4 + [hbm],
        out_specs=(
            pl.BlockSpec(memory_space=pltpu.VMEM),
            pl.BlockSpec(memory_space=pltpu.VMEM),
        ),
        scratch_shapes=[
            vmem((2, 8, 36, 16, 128), BF),
            vmem((2, 8, 4, ROWS, N), BF),
            vmem((2, N, N), F32),
            vmem((2, 8, 4, ROWS, N), BF),
            vmem((192, 192), BF),
            vmem((192, 192), BF),
            vmem((2 * N, 2 * N), BF),
            vmem((2 * N, 2 * N), BF),
            vmem((256, 256), BF),
            vmem((N, N), F32),
            vmem((2, 4, N, N), BF),
            vmem((192, 16, N), BF),
            vmem((12, 256, N), BF),
            vmem((4, 2, N, N), BF),
            vmem((4, 2, N, N), F32),
            vmem((2, 8, 192, N), BF),
            vmem((192, 16, N), BF),
            vmem((12, 256, N), BF),
            vmem((2, 4, N, N), BF),
            vmem((2 * N, N), BF),
            vmem((2 * N, N), BF),
            vmem((N, 2 * N), BF),
            vmem((8, 256), F32),
            vmem((8, 8, 256), F32),
            vmem((4, 16, N), F32),
            vmem((16, N), F32),
            vmem((256, N), F32),
            vmem((16, 12, N), F32),
            vmem((16, 12, N), F32),
            vmem((16, N), BF),
            vmem((2, 256, N), BF),
            vmem((N, N), F32),
            vmem((N, N), F32),
            vmem((256, 256), F32),
            vmem((256, 256), BF),
            vmem((8, 32, 128), F32),
            vmem((256, 128), F32),
            vmem((16, 16, 256), BF),
            dma((1,)), dma((4,)),
            dma((1,)), dma((4,)),
            dma((1,)), dma((1,)),
            dma((4,)), dma((1,)),
            dma((1,)), dma((1,)),
            dma((1,)), dma((1,)),
            dma((1,)), dma((1,)),
            dma((1,)), dma((4,)),
            dma((1,)), dma((PARTS,)),
            dma((1,)), dma((PARTS,)),
            dma((1,)), dma((1,)),
            dma((1,)), dma((1,)),
            dma((5,)),
        ],
        compiler_params=pltpu.CompilerParams(
            collective_id=0, has_side_effects=True, vmem_limit_bytes=56 * 1024 * 1024
        ),
    )(
        tiled, point_charge.reshape(1, 256), charge_place, charge_slab.reshape(1, 256),
        ionic_field, table,
    )
    out = out.reshape(2, 8, 144, 4, 128).transpose(0, 1, 3, 2, 4)
    return out.reshape(2, 8, 4, ROWS * N), sub


def solution(mesh):
    placed = (
        P(None, "band", None, "ga"),
        P("ga", None),
        P(("band", "ga")),
        P(None, ("band", "ga")),
        P(("band", "ga"), None),
    )
    mapped = jax.shard_map(
        shards,
        mesh=mesh,
        in_specs=(P(None, None, None),) + placed,
        out_specs=(P(None, "band", None, "ga"), P(None, "band", "ga")),
        check_vma=False,
    )
    return functools.partial(mapped, tables())
```

```python
import functools

import jax
import jax.numpy as jnp
import ml_dtypes
import numpy as np
from jax import lax
from jax.experimental import pallas as pl
from jax.experimental.pallas import tpu as pltpu
from jax.sharding import PartitionSpec as P

N = 384
ROWS = 48
BF = jnp.bfloat16
F32 = jnp.float32
MESH = pl.DeviceIdType.MESH


def tables():
    indices = np.arange(N, dtype=np.int32)
    phases = indices[:, None] * indices[None, :] % N
    angles = phases.astype(np.float32) * np.float32(2.0 * np.pi / N)
    factor = np.float32(1.0) / np.sqrt(np.float32(N))
    both = np.stack([np.cos(angles) * factor, np.sin(angles) * factor])
    return both.astype(ml_dtypes.bfloat16).astype(np.float32)


def dot(a, b):
    return jnp.dot(a, b, preferred_element_type=F32)


def dot_nt(a, b):
    return lax.dot_general(a, b, (((1,), (1,)), ((), ())), preferred_element_type=F32)


def split(value):
    high = value.astype(BF)
    return high, (value - high.astype(F32)).astype(BF)


def gaussian(distance):
    return jnp.exp(-distance * distance / 4.5)


SHIFTS = (
    (0, 1), (1, 0), (0, 3), (3, 0), (2, 2), (1, 1), (3, 3), (1, 3),
    (3, 1), (0, 2), (2, 0), (1, 2), (2, 1), (3, 2), (2, 3),
)
PARTS = 4
PART = 12 // PARTS


def each(low, high, body):
    def step(k, c):
        body(k)
        return c

    lax.fori_loop(low, high, step, 0)


def at(start, size, step):
    return pl.ds(pl.multiple_of(start * size, step), size)


def place_of(row):
    m = row >> 4
    plane = (m * 11) >> 5
    return ((row & 15) * 3 + m - 3 * plane) * 4 + plane


def kernel(
    waves, charge, place, slab_in, ionic, tab_in, out, sub,
    xin, w1, tab, rows_in, spread, gather, m1, m2, perm, kin, zb, w2, xw, phi, wide, ph, p2, xp, ab, fs, ts, bs,
    chs, ch, ios, iop, pot, pt, rsb, own, pf, vyx, vxy, gt, gb, sa, st, sb,
    zi_s, zi_r, zo_s, zo_r, ch_s, ch_r, io_s, io_r, rs_s, rs_r, ag_s, ag_r,
    sp_s, sp_r, sf_s, sf_r, xw_s, xw_r, xp_s, xp_r, sa_s, sa_r, sb_s, sb_r, loc,
):
    b = lax.axis_index("band")
    g = lax.axis_index("ga")
    z = g // 2
    h = lax.rem(g, 2)
    sibling = g + 1 - 2 * h
    b_y = b // 4
    b_x = lax.rem(b, 4)

    def ga_peer(k):
        return lax.rem(g + k, 8)

    def band_peer(k):
        return lax.rem(b + k, 16)

    def shifted(dy, dx):
        return lax.rem(b_y + dy, 4) * 4 + lax.rem(b_x + dx, 4)

    def remote(src, dst, send, recv, band, ga):
        return pltpu.make_async_remote_copy(
            src_ref=src, dst_ref=dst, send_sem=send, recv_sem=recv,
            device_id=(band, ga), device_id_type=MESH,
        )

    barrier = pltpu.get_barrier_semaphore()
    each(1, 8, lambda k: pl.semaphore_signal(
        barrier, inc=1, device_id=(b, ga_peer(k)), device_id_type=MESH))
    each(1, 16, lambda k: pl.semaphore_signal(
        barrier, inc=1, device_id=(band_peer(k), g), device_id_type=MESH))

    def load(n):
        return pltpu.make_async_copy(
            waves.at[:, pl.ds(2 * n, 2)], xin.at[:, pl.ds(2 * n, 2)], loc.at[n]
        )

    def load_tab():
        return pltpu.make_async_copy(tab_in, tab, loc.at[4])

    for n in range(4):
        load(n).start()
    load_tab().start()

    lead = lax.broadcasted_iota(jnp.int32, (192, 192), 0)
    last = lax.broadcasted_iota(jnp.int32, (192, 192), 1)
    spread[...] = jnp.where(last == place_of(lead), 1.0, 0.0).astype(BF)
    gather[...] = jnp.where(lead == place_of(last), 1.0, 0.0).astype(BF)

    def to_planes(n):
        load(n).wait()
        for core in range(2):
            for x in range(3):
                both = jnp.concatenate(
                    [xin[c, 2 * n + core, 12 * x : 12 * x + 12].reshape(192, 128) for c in range(2)],
                    axis=1,
                )
                rows = dot(spread[...], both).astype(BF)
                for m in range(12):
                    part = m % 3 * 128
                    for c in range(2):
                        w1[c, 2 * n + core, m // 3, 16 * x : 16 * x + 16, part : part + 128] = (
                            rows[16 * m : 16 * m + 16, 128 * c : 128 * c + 128]
                        )

    def from_planes(n):
        for core in range(2):
            for x in range(3):
                both = jnp.concatenate(
                    [
                        jnp.concatenate(
                            [
                                rows_in[
                                    c, 2 * n + core, m // 3, 16 * x : 16 * x + 16,
                                    m % 3 * 128 : m % 3 * 128 + 128,
                                ]
                                for m in range(12)
                            ],
                            axis=0,
                        )
                        for c in range(2)
                    ],
                    axis=1,
                )
                rows = dot(gather[...], both).astype(BF)
                for c in range(2):
                    out[c, 2 * n + core, 12 * x : 12 * x + 12] = rows[
                        :, 128 * c : 128 * c + 128
                    ].reshape(12, 16, 128)

    chs[0:1] = charge[...]
    chs[1:4] = place[...]
    chs[4:5] = slab_in[...].astype(F32)
    chs[5:8] = jnp.zeros((3, 256), F32)
    each(0, 4, to_planes)

    to = lax.broadcasted_iota(jnp.int32, (256, 256), 0)
    of = lax.broadcasted_iota(jnp.int32, (256, 256), 1)
    perm[...] = jnp.where(
        ((to >> 4) == (of & 15)) & ((to & 15) == (of >> 4)), 1.0, 0.0
    ).astype(BF)
    def turn(p):
        for x in range(3):
            block = w1[:, :, p, 16 * x : 16 * x + 16, :].reshape(256, N)
            turned = dot(perm[...], block).astype(BF).reshape(16, 16, N)
            w2[pl.ds(ROWS * p + 16 * x, 16)] = turned

    pl.semaphore_wait(barrier, 22)

    def local(src, dst, sem):
        pltpu.make_async_copy(src, dst, sem).start()

    def await_bytes(like, sem):
        pltpu.make_async_copy(like, like, sem).wait()

    def ch_send(target):
        remote(chs, ch.at[g], ch_s.at[0], ch_r.at[0], b, target).start()

    io_sends = lax.rem(g, 4) == b_y
    io_half = g // 4
    io_source = 4 * h + b_y

    def io_copy(plane):
        return remote(
            ios.at[plane], iop, io_s.at[plane], io_r.at[0], b, 2 * plane + io_half
        )

    def zi_send(n, target):
        remote(
            w1.at[:, 2 * n + lax.rem(target, 2), target // 2],
            zb.at[:, n, at(g, ROWS, 16), :], zi_s.at[0], zi_r.at[n], b, target,
        ).start()

    def zo_send(n, target):
        remote(
            ab.at[:, n, at(target, ROWS, 16), :],
            rows_in.at[:, 2 * n + h, z], zo_s.at[0], zo_r.at[n], b, target,
        ).start()

    def row_sends(q, src, dst, send, recv):
        def to(target):
            return src.at[pl.ds(ROWS * q + PART * target, PART)], dst.at[pl.ds(PART * q, PART), at(b, 16, 16), :]

        for dy, dx in SHIFTS:
            target = shifted(dy + h * (dx - dy), dx + h * (dy - dx))
            one, other = to(target)
            remote(one, other, send.at[0], recv.at[q], target, g).start()
        one, other = to(b)
        local(one, other, recv.at[q])

    def sp_copy(half):
        return remote(pf.at[half], pf.at[half], sp_s.at[0], sp_r.at[0], b, sibling)

    def sf_copy(n, part, core):
        return remote(
            phi.at[n, part, at(1 - core, 192, 16), :], ph.at[part, 2 * n + core],
            sf_s.at[0], sf_r.at[n], b, sibling,
        )

    each(1, 8, lambda k: ch_send(ga_peer(k)))
    local(chs, ch.at[g], ch_r.at[0])
    def zi_all(n):
        each(1, 8, lambda k: zi_send(n, ga_peer(k)))
        local(w1.at[:, 2 * n + h, z], zb.at[:, n, at(g, ROWS, 16), :], zi_r.at[n])

    zi_all(0)

    def send_waves(q):
        row_sends(q, w2, xw, xw_s, xw_r)

    turn(0)
    send_waves(0)
    each(1, 4, zi_all)
    turn(1)
    send_waves(1)
    each(2, 4, turn)

    @pl.when(io_sends)
    def _():
        for j in range(4):
            @pl.when(b_x == j)
            def _(j=j):
                for plane in range(4):
                    rows = ionic[12 * j : 12 * j + 12, plane * N : (plane + 1) * N]
                    ios[plane] = jnp.concatenate([rows, jnp.zeros((4, N), F32)], axis=0)
        for plane in range(4):
            @pl.when(2 * plane + io_half != g)
            def _(plane=plane):
                io_copy(plane).start()

    load_tab().wait()
    c = tab[0].astype(BF)
    s = tab[1].astype(BF)
    m1[0:N, 0:N] = c
    m1[0:N, N : 2 * N] = s
    m1[N : 2 * N, 0:N] = -s
    m1[N : 2 * N, N : 2 * N] = c
    m2[0:N, 0:N] = c
    m2[0:N, N : 2 * N] = -s
    m2[N : 2 * N, 0:N] = s
    m2[N : 2 * N, N : 2 * N] = c

    def frequency(indices):
        return jnp.where(indices < N // 2, indices, indices - N).astype(F32)

    fx = frequency(lax.broadcasted_iota(jnp.int32, (N, N), 0))
    fy = frequency(lax.broadcasted_iota(jnp.int32, (N, N), 1))
    kin[...] = 2.0 * (fx * fx / (N * N) + fy * fy / (N * N))

    await_bytes(ch, ch_r.at[0])
    pot[...] = jnp.zeros((256, N), F32)

    def add_charges(source):
        rows = ch[source]
        q, u, v, w, slab = (rows[i : i + 1] for i in range(5))
        r = lax.broadcasted_iota(jnp.int32, (256, 256), 0)
        y = 192 * h + 12 * (r >> 4) + (r & 15)
        weight = q * gaussian(z.astype(F32) - 4.0 * w)
        inside = ((y * 1366) >> 16).astype(F32) == slab
        gy = gaussian(y.astype(F32) - (slab * 48.0 + 48.0 * v)) * weight
        gy = jnp.where(inside, gy, 0.0)
        x = lax.broadcasted_iota(jnp.int32, (N, 256), 0).astype(F32)
        gx = gaussian(x - 384.0 * u)
        yh, yl = split(gy)
        xh, xl = split(gx)
        pot[...] += dot_nt(yh, xh) + (dot_nt(yh, xl) + dot_nt(yl, xh))

    def add_two(i):
        add_charges(2 * i)
        add_charges(2 * i + 1)

    each(0, 4, add_two)

    for j in range(16):
        pt[j] = pot[16 * j : 16 * j + 12, :]

    def rs_send(target):
        remote(
            pt.at[target], rsb.at[b], rs_s.at[0], rs_r.at[0], target, g
        ).start()

    each(1, 16, lambda k: rs_send(band_peer(k)))
    local(pt.at[b], rsb.at[b], rs_r.at[0])
    send_waves(2)

    def forward(n):
        await_bytes(zb.at[:, n], zi_r.at[n])
        both = jnp.concatenate([zb[0, n], zb[1, n]], axis=1)
        fs[0:N] = dot(both, m1[:, 0:N]).astype(BF)
        fs[N : 2 * N] = dot(both, m1[:, N : 2 * N]).astype(BF)
        for part in range(2):
            space = dot(m2[part * N : (part + 1) * N], fs[...])
            wide[n, part] = space
            phi[n, part] = space.astype(BF)
            sf_copy(n, part, h).start()
        for part in range(2):
            ph[part, 2 * n + h] = phi[n, part, at(h, 192, 16), :]

    each(0, 2, forward)

    await_bytes(rsb, rs_r.at[0])

    @pl.when(io_source == g)
    def _():
        iop[...] = ios[z]

    @pl.when(io_source != g)
    def _():
        io_copy(z).wait_recv()

    piece = iop[0:12]
    for k in range(16):
        piece = piece + rsb[k]
    own[...] = jnp.concatenate([piece, jnp.zeros((4, N), F32)], axis=0).astype(BF)

    def ag_send(target):
        remote(own, pf.at[h, at(b, 16, 16), :], ag_s.at[0], ag_r.at[0], target, g).start()

    each(1, 16, lambda k: ag_send(band_peer(k)))
    local(own, pf.at[h, at(b, 16, 16), :], ag_r.at[0])
    send_waves(3)
    each(2, 4, forward)

    each(0, 4, lambda n: await_bytes(ph.at[:, n], sf_r.at[n]))

    def turn_field(p):
        for x in range(3):
            block = ph[:, :, at(3 * p + x, 16, 16), :].reshape(256, N)
            p2[at(3 * p + x, 16, 16)] = dot(perm[...], block).astype(BF).reshape(16, 16, N)

    for q in range(PARTS):
        turn_field(q)
        row_sends(q, p2, xp, xp_s, xp_r)
        if q == 1:
            await_bytes(pf.at[h], ag_r.at[0])
            sp_copy(h).start()

    sp_copy(1 - h).wait_recv()
    for half in range(2):
        def join(q, half=half):
            two = pf[half, at(q, 32, 16), :].astype(F32)
            dst = pl.ds(pl.multiple_of(192 * half + 24 * q, 8), 24)
            vyx[dst, :] = jnp.concatenate([two[0:12], two[16:28]], axis=0)

        each(0, 8, join)
    vxy[...] = vyx[...].T

    def backward(n):
        for part in range(2):
            ts[part * N : (part + 1) * N] = (wide[n, part] * vxy[...]).astype(BF)
        for part in range(2):
            bs[:, part * N : (part + 1) * N] = dot(
                m1[part * N : (part + 1) * N], ts[...]
            ).astype(BF)
        for part in range(2):
            recip = dot(bs[...], m2[:, part * N : (part + 1) * N])
            ab[part, n] = (kin[...] * zb[part, n].astype(F32) + recip).astype(BF)
        each(1, 8, lambda k: zo_send(n, ga_peer(k)))
        local(ab.at[:, n, at(g, ROWS, 16), :], rows_in.at[:, 2 * n + h, z], zo_r.at[n])

    each(0, 4, backward)

    def gram(data, q, weights):
        rows = [data[PART * q + i] for i in range(PART)]
        scaled = [(r.astype(F32) * w).astype(BF) for r, w in zip(rows, weights)]
        gt[...] += dot_nt(jnp.concatenate(rows, axis=1), jnp.concatenate(scaled, axis=1))

    gt[...] = jnp.zeros((256, 256), F32)

    def gram_waves(q):
        await_bytes(xw.at[pl.ds(PART * q, PART)], xw_r.at[q])
        x = [ROWS * g + PART * b + i for i in range(PART)]
        gram(xw, q, [kin[pl.ds(i, 1), :] for i in x])

    each(0, PARTS, gram_waves)

    await_bytes(w1.at[:, pl.ds(0, 7)], zi_s.at[0])
    await_bytes(ph.at[:, pl.ds(0, 4)], sf_s.at[0])
    await_bytes(ch.at[pl.ds(0, 7)], ch_s.at[0])
    await_bytes(rsb.at[pl.ds(0, 15)], rs_s.at[0])
    await_bytes(pf.at[0, pl.ds(0, 240)], ag_s.at[0])
    await_bytes(w2.at[pl.ds(0, 180)], xw_s.at[0])
    sp_copy(h).wait_send()

    @pl.when(io_sends)
    def _():
        for plane in range(4):
            @pl.when(2 * plane + io_half != g)
            def _(plane=plane):
                io_copy(plane).wait_send()

    def finish(n):
        await_bytes(rows_in.at[:, pl.ds(2 * n, 2)], zo_r.at[n])
        from_planes(n)

    def gram_fields(q):
        await_bytes(xp.at[pl.ds(PART * q, PART)], xp_r.at[q])
        x = [192 * h + ROWS * q + PART * b + i for i in range(PART)]
        gram(xp, q, [vxy[pl.ds(i, 1), :] for i in x])

    gram_fields(0)
    gram_fields(1)
    gram_fields(2)
    each(0, 2, finish)
    gram_fields(3)

    gb[...] = gt[...].astype(BF)

    def sb_send(target):
        remote(
            gb.at[at(target, 16, 16), :], sb.at[b], sb_s.at[0], sb_r.at[0], target, g
        ).start()

    each(1, 16, lambda k: sb_send(band_peer(k)))
    local(gb.at[at(b, 16, 16), :], sb.at[b], sb_r.at[0])
    await_bytes(p2.at[pl.ds(0, 180)], xp_s.at[0])
    finish(2)
    await_bytes(sb, sb_r.at[0])
    total = sb[0].astype(F32)
    for k in range(1, 16):
        total = total + sb[k].astype(F32)
    st[...] = jnp.concatenate([total, jnp.zeros((112, 256), F32)], axis=0).T.astype(BF)

    def sa_send(target):
        remote(
            st.at[at(target, 32, 16), :], sa.at[g], sa_s.at[0], sa_r.at[0], b, target
        ).start()

    each(1, 8, lambda k: sa_send(ga_peer(k)))
    local(st.at[at(g, 32, 16), :], sa.at[g], sa_r.at[0])
    finish(3)
    await_bytes(w1.at[:, pl.ds(0, 7)], zo_s.at[0])
    await_bytes(sb.at[pl.ds(0, 15)], sb_s.at[0])
    await_bytes(sa, sa_r.at[0])
    block = sa[0].astype(F32)
    for k in range(1, 8):
        block = block + sa[k].astype(F32)
    block = jnp.concatenate([block, jnp.zeros((96, 128), F32)], axis=0).T[0:16]
    row = lax.broadcasted_iota(jnp.int32, (128, 128), 0)
    col = lax.broadcasted_iota(jnp.int32, (128, 128), 1)
    lane = ((col >> 3) << 4) + (col & 7)
    valid = col < 16
    pick_re = jnp.where(valid & (row == lane), 1.0, 0.0)
    pick_im = jnp.where(valid & (row == lane + 8), 1.0, 0.0)

    def pick(rows, which):
        return jnp.dot(rows, which, precision=lax.Precision.HIGHEST, preferred_element_type=F32)

    inverse_cells = 1.0 / (4 * N * N)
    rr, ri = pick(block, pick_re), pick(block, pick_im)
    sub[0] = ((rr[0:8] + ri[8:16]) * inverse_cells)[:, 0:16]
    sub[1] = ((ri[0:8] - rr[8:16]) * inverse_cells)[:, 0:16]

    await_bytes(sa.at[pl.ds(0, 7)], sa_s.at[0])


def shards(table, waves, ionic_field, point_charge, charge_place, charge_slab):
    tiled = waves.reshape(2, 8, 4, 144, 128).transpose(0, 1, 3, 2, 4).reshape(2, 8, 36, 16, 128)
    dma = pltpu.SemaphoreType.DMA
    vmem = pltpu.VMEM
    hbm = pl.BlockSpec(memory_space=pltpu.MemorySpace.HBM)
    out, sub = pl.pallas_call(
        kernel,
        out_shape=(
            vmem((2, 8, 36, 16, 128), BF),
            vmem((2, 8, 16), F32),
        ),
        in_specs=[hbm] + [pl.BlockSpec(memory_space=pltpu.VMEM)] * 4 + [hbm],
        out_specs=(
            pl.BlockSpec(memory_space=pltpu.VMEM),
            pl.BlockSpec(memory_space=pltpu.VMEM),
        ),
        scratch_shapes=[
            vmem((2, 8, 36, 16, 128), BF),
            vmem((2, 8, 4, ROWS, N), BF),
            vmem((2, N, N), F32),
            vmem((2, 8, 4, ROWS, N), BF),
            vmem((192, 192), BF),
            vmem((192, 192), BF),
            vmem((2 * N, 2 * N), BF),
            vmem((2 * N, 2 * N), BF),
            vmem((256, 256), BF),
            vmem((N, N), F32),
            vmem((2, 4, N, N), BF),
            vmem((192, 16, N), BF),
            vmem((12, 256, N), BF),
            vmem((4, 2, N, N), BF),
            vmem((4, 2, N, N), F32),
            vmem((2, 8, 192, N), BF),
            vmem((192, 16, N), BF),
            vmem((12, 256, N), BF),
            vmem((2, 4, N, N), BF),
            vmem((2 * N, N), BF),
            vmem((2 * N, N), BF),
            vmem((N, 2 * N), BF),
            vmem((8, 256), F32),
            vmem((8, 8, 256), F32),
            vmem((4, 16, N), F32),
            vmem((16, N), F32),
            vmem((256, N), F32),
            vmem((16, 12, N), F32),
            vmem((16, 12, N), F32),
            vmem((16, N), BF),
            vmem((2, 256, N), BF),
            vmem((N, N), F32),
            vmem((N, N), F32),
            vmem((256, 256), F32),
            vmem((256, 256), BF),
            vmem((8, 32, 128), BF),
            vmem((256, 128), BF),
            vmem((16, 16, 256), BF),
            dma((1,)), dma((4,)),
            dma((1,)), dma((4,)),
            dma((1,)), dma((1,)),
            dma((4,)), dma((1,)),
            dma((1,)), dma((1,)),
            dma((1,)), dma((1,)),
            dma((1,)), dma((1,)),
            dma((1,)), dma((4,)),
            dma((1,)), dma((PARTS,)),
            dma((1,)), dma((PARTS,)),
            dma((1,)), dma((1,)),
            dma((1,)), dma((1,)),
            dma((5,)),
        ],
        compiler_params=pltpu.CompilerParams(
            collective_id=0, has_side_effects=True, vmem_limit_bytes=56 * 1024 * 1024
        ),
    )(
        tiled, point_charge.reshape(1, 256), charge_place, charge_slab.reshape(1, 256),
        ionic_field, table,
    )
    out = out.reshape(2, 8, 144, 4, 128).transpose(0, 1, 3, 2, 4)
    return out.reshape(2, 8, 4, ROWS * N), sub


def solution(mesh):
    placed = (
        P(None, "band", None, "ga"),
        P("ga", None),
        P(("band", "ga")),
        P(None, ("band", "ga")),
        P(("band", "ga"), None),
    )
    mapped = jax.shard_map(
        shards,
        mesh=mesh,
        in_specs=(P(None, None, None),) + placed,
        out_specs=(P(None, "band", None, "ga"), P(None, "band", "ga")),
        check_vma=False,
    )
    return functools.partial(mapped, tables())
```
